512 devices in a mesh: tm: 16 (over z), height: 8 (over y, core), width: 4 (over x).
Axes of the slice: x: 4, y: 4, z: 16, core: 2. Of those that a mesh axis runs over, the one named last changes fastest.
Arguments:
- video: bfloat16 [3, 64, 256, 1024], P(None, 'tm', 'height', 'width'), may hold values from -6 to 6
- w_conv: bfloat16 [3, 3, 3, 24, 128], replicated, may hold values from -0.25 to 0.25
- w_merge: bfloat16 [512, 512], replicated, may hold values from -0.25 to 0.25
- w_qkv: bfloat16 [512, 1536], replicated, may hold values from -0.25 to 0.25
- w_out: bfloat16 [512, 512], replicated, may hold values from -0.25 to 0.25
Outputs:
- encoded: bfloat16 [32, 64, 256, 512], P('tm', 'height', 'width')
The draws below stay inside these ranges and needn't reach their ends.
All inputs are finite; a program needn't handle non-finite values.
Results may differ from the reference program's by a relative error of at most 0.013.
Values may be sent and summed in bfloat16 or wider, within the bound.
A program may use at most 192 MiB of HBM per device.

```python
import math
import jax
import jax.numpy as jnp
from jax import lax

CH = 128
D = 512
HEADS = 8
FRAMES = 64
PIX_ROWS = 256
PIX_COLS = 1024


def steps_of(key, dims, split, low, largest):
    factor_of = 1.0
    for dim, shards_of in split:
        draws = jax.random.uniform(jax.random.fold_in(jax.random.fold_in(key, 6), dim), (shards_of,), jnp.float32, low / len(split), largest / len(split))
        factor_of = factor_of * jnp.repeat(jnp.exp(draws), dims[dim] // shards_of).reshape((-1,) + (1,) * (len(dims) - 1 - dim))
    return factor_of


def noise(stream_key, dims, scale, most, pieces=(), kind=jnp.bfloat16):
    result = jax.random.normal(stream_key, dims, jnp.float32) * scale
    if len(pieces) > 0:
        result = steps_of(stream_key, dims, pieces, -0.22, 0.18) * result
    return jnp.clip(result, min=-most, max=most).astype(kind)


def setup_inputs(seed: int = 0) -> dict:
    arg_keys = jax.random.split(jax.random.key(seed), 6)
    return {
        "video": noise(arg_keys[0], (3, FRAMES, PIX_ROWS, PIX_COLS), 1.0, 6.0, ((1, 16), (2, 8), (3, 4))),
        "w_conv": noise(arg_keys[1], (3, 3, 3, 24, CH), 648 ** -0.5, 0.25),
        "w_merge": noise(arg_keys[2], (D, D), D ** -0.5, 0.25),
        "w_qkv": noise(arg_keys[3], (D, 3 * D), D ** -0.5, 0.25),
        "w_out": noise(arg_keys[4], (D, D), D ** -0.5, 0.25),
    }


def wavelet(video):
    values = video.astype(jnp.float32)
    chans, frames, rows, cols = values.shape
    values = values.reshape(chans, frames // 2, 2, rows // 2, 2, cols // 2, 2)
    first, second = (values[:, :, 0], values[:, :, 1])
    values = jnp.stack([first + second, first - second], axis=1)
    first, second = (values[:, :, :, :, 0], values[:, :, :, :, 1])
    values = jnp.stack([first + second, first - second], axis=2)
    first, second = (values[..., 0], values[..., 1])
    values = jnp.stack([first + second, first - second], axis=3)
    values = values.reshape(chans * 8, frames // 2, rows // 2, cols // 2)
    return (values * (1.0 / math.sqrt(8.0))).astype(jnp.bfloat16)

def convolve(padded, weight, frames, rows, cols):
    total = jnp.zeros((weight.shape[-1], frames * rows * cols), jnp.float32)
    for step_t in range(3):
        for step_h in range(3):
            for step_w in range(3):
                window = padded[:, step_t:step_t + frames, step_h:step_h + rows, step_w:step_w + cols]
                window = window.reshape(padded.shape[0], -1)
                total = total + lax.dot_general(weight[step_t, step_h, step_w], window, (((0,), (0,)), ((), ())), preferred_element_type=jnp.float32)
    return jax.nn.silu(total).reshape(-1, frames, rows, cols).astype(jnp.bfloat16)

def to_tokens(features):
    chans, frames, rows, cols = features.shape
    merged = features.reshape(chans, frames, rows // 2, 2, cols // 2, 2)
    merged = merged.transpose(1, 2, 4, 0, 3, 5)
    return merged.reshape(frames, rows // 2, cols // 2, chans * 4)

def project_in(tokens, w_merge):
    width = w_merge.shape[0]
    latent = jnp.dot(tokens.reshape(-1, width), w_merge, preferred_element_type=jnp.float32).astype(jnp.bfloat16)
    wide = latent.astype(jnp.float32)
    meansq = lax.optimization_barrier(jnp.mean(wide * wide, axis=-1, keepdims=True))
    normed = (wide * lax.rsqrt(meansq + 1e-06)).astype(jnp.bfloat16)
    return (latent.reshape(tokens.shape), normed.reshape(tokens.shape))

def attend(combined, heads):
    frames, places, triple = combined.shape
    width = triple // 3
    size = width // heads
    query = combined[..., :width].reshape(frames, places, heads, size).astype(jnp.float32)
    keys = combined[..., width:2 * width].reshape(frames, places, heads, size).astype(jnp.float32)
    values = combined[..., 2 * width:].reshape(frames, places, heads, size).astype(jnp.float32)
    scores = jnp.einsum('tphd,sphd->phts', query, keys) * size ** (-0.5)
    allowed = jnp.arange(frames)[:, None] >= jnp.arange(frames)[None, :]
    scores = jnp.where(allowed, scores, jnp.float32(-1e+30))
    top = lax.optimization_barrier(jnp.max(scores, axis=-1, keepdims=True))
    expon = jnp.exp(scores - top)
    probs = (expon / lax.optimization_barrier(jnp.sum(expon, axis=-1, keepdims=True))).astype(jnp.bfloat16)
    mixed = jnp.einsum('phts,sphd->tphd', probs.astype(jnp.float32), values)
    return mixed.reshape(frames, places, width).astype(jnp.bfloat16)

def finish(latent, mixed, w_out):
    width = w_out.shape[0]
    branch = jnp.dot(mixed.reshape(-1, width), w_out, preferred_element_type=jnp.float32)
    total = latent.reshape(-1, width).astype(jnp.float32) + branch
    return total.reshape(latent.shape).astype(jnp.bfloat16)

def reference(video, w_conv, w_merge, w_qkv, w_out):
    bands = wavelet(video)
    subs, frames, rows, cols = bands.shape
    padded = jnp.pad(bands, ((0, 0), (2, 0), (1, 1), (1, 1)))

    def one_frame(index):
        window = lax.dynamic_slice_in_dim(padded, index, 3, 1)
        return convolve(window, w_conv, 1, rows, cols)[:, 0]
    features = lax.map(one_frame, jnp.arange(frames, dtype=jnp.int32))
    features = features.transpose(1, 0, 2, 3)
    width = w_merge.shape[0]

    def one_row(index):
        strip = lax.dynamic_slice_in_dim(features, (index * 2).astype(jnp.int32), 2, 2)
        tokens = to_tokens(strip).reshape(frames, -1, width)
        latent, normed = project_in(tokens, w_merge)
        combined = jnp.dot(normed.reshape(-1, width), w_qkv, preferred_element_type=jnp.float32).astype(jnp.bfloat16)
        mixed = attend(combined.reshape(frames, -1, 3 * width), HEADS)
        return finish(latent, mixed, w_out)
    rows_out = lax.map(one_row, jnp.arange(rows // 2, dtype=jnp.int32))
    return rows_out.transpose(1, 0, 2, 3)
```

```python
import functools
import math

import jax
import jax.numpy as jnp
from jax import lax
from jax.experimental import pallas as pl
from jax.experimental.pallas import tpu as pltpu
from jax.sharding import PartitionSpec as P

HEADS = 8

CHANS, FRAMES, ROWS, COLS = 3, 4, 32, 256
TIMES = FRAMES // 2
BLOCK = 4
TALL, WIDE = ROWS // BLOCK, COLS // BLOCK
SPAN = 16
ACROSS = WIDE // SPAN
UNIT = 32
STEPS = 80
UNITS = 20
WIDTH = 512
PARTS = 2
LINES = 64
AHEAD = 16
COPIES = 8
DENSE = 96
SPARE = 32
BF16 = jnp.bfloat16
MESH = pl.DeviceIdType.MESH


class Plan:
    def __init__(self, ring):
        self.ring = ring
        self.times = ring * TIMES
        self.blocks = ring // 2
        self.tall = TALL * ACROSS // self.blocks
        self.units = TIMES * (self.tall + 1) // PARTS
        self.tokens = self.times * SPAN
        self.group = self.times * 4
        self.frames = self.times // 2


def index(count):
    return lax.broadcasted_iota(jnp.int32, (count, 1), 0)


def among(value, low, high):
    return (value >= low) & (value < high)


def one_hot(target, width):
    lane = lax.broadcasted_iota(jnp.int32, (target.shape[0], width), 1)
    return jnp.where(lane == target, 1.0, 0.0).astype(BF16)


def strip_rows():
    row = index(128)
    side, rest = row >> 5, row & 31
    target = (rest >> 1) * ROWS + (1 - side) * (ROWS - 2) + (rest & 1)
    used = (rest < 2 * CHANS * FRAMES) & (side < 2)
    return one_hot(jnp.where(used, target, -1), CHANS * FRAMES * ROWS)


def unit_rows():
    row = index(UNITS * UNIT)
    unit, k = row >> 5, row & 31
    late = jnp.where(unit >= TALL + 1, 1, 0)
    plane = (k >> 3) * FRAMES + 2 * late + ((k >> 2) & 1)
    at = (unit - late * (TALL + 1)) * BLOCK + (k & 3) - 2
    used = (unit < 2 * (TALL + 1)) & (k < 24)
    main = jnp.where(used & among(at, 0, ROWS), plane * ROWS + at, -1)
    halo = jnp.where(at < 0, plane * 2 + at + 2, 32 + plane * 2 + at - ROWS)
    halo = jnp.where(used & ~among(at, 0, ROWS), halo, -1)
    return one_hot(main, CHANS * FRAMES * ROWS), one_hot(halo, 128)


def edge_columns():
    row = index(32)
    line = row & 15
    return one_hot(jnp.where(line < 2, line + (1 - (row >> 4)) * (COLS - 2), -1), COLS)


def block_columns():
    row = index(BLOCK * STEPS)
    c = sum(jnp.where(row >= n * STEPS, 1, 0) for n in range(1, BLOCK))
    x = row - c * STEPS
    at = x * BLOCK + c - 2
    main = jnp.where(among(at, 0, COLS), at, -1)
    halo = jnp.where(at < 0, at + 2, jnp.where(x <= WIDE, 16 + at - COLS, -1))
    return one_hot(main, COLS), one_hot(jnp.where(among(at, 0, COLS), -1, halo), 32)


def unit_lanes():
    row = index(512)
    k = row & 31
    target = ((row >> 5) & 3) * 128 + (row >> 7) * 24 + k
    return one_hot(jnp.where(k < 24, target, -1), 512)


def part_rows(plan):
    row = index(LINES)
    late = jnp.where(row >= AHEAD, 1, 0)
    below = row - late * AHEAD
    third = (below * 171) >> 9
    piece = below - 3 * third

    def source(item):
        unit = (item * 3856) >> 16
        return unit * 32 + item - unit * (SPAN + 1)

    width = plan.units * 32
    every = [one_hot(source(row + 5 * late), width)]
    used = (late == 1) | (below < 15)
    for n in range(3):
        item = jnp.where(late == 1, 69, 16) + third
        every.append(one_hot(jnp.where(used & (piece == n), source(item), -1), width))
    return jnp.concatenate(every, axis=0)


def spare_lanes():
    lane = index(128)
    every = [one_hot(jnp.where(lane < DENSE, lane, -1), 128)]
    for piece in range(3):
        at = lane - piece * SPARE
        every.append(one_hot(jnp.where(among(at, 0, SPARE), DENSE + at, -1), 128))
    return jnp.concatenate(every, axis=0)


def part_lanes():
    lane = index(128)
    every = [one_hot(jnp.where(lane < DENSE, lane, -1), 128)]
    for piece in range(3):
        every.append(one_hot(jnp.where(lane >= DENSE, lane - DENSE + piece * SPARE, -1), 128))
    return jnp.concatenate(every, axis=1)


def window_rows(first, units, lines):
    row = index(units * 32)
    item = (first + (row >> 5)) * (SPAN + 1) + (row & 15) + ((row >> 4) & 1)
    main = jnp.where(item < 16, item, jnp.where(among(item, 21, 69), item - 5, -1))
    total = one_hot(main, 4 * lines)
    rest = jnp.where(item < 69, 3 * (item - 16), AHEAD + 3 * (item - 69))
    for piece in range(3):
        at = (1 + piece) * lines + rest + piece
        total += one_hot(jnp.where(main < 0, at, -1), 4 * lines)
    return total


def tap_signs(out_pixel):
    i, j = divmod(out_pixel, 2)
    row = index(512)
    lane = row & 127
    c = sum(jnp.where(lane >= n * 24, 1, 0) for n in range(1, BLOCK))
    k = lane - c * 24
    up, along = ((row >> 8) & 1) * 4 + (k & 3), ((row >> 7) & 1) * 4 + c
    q, r = (up >> 1) - i, (along >> 1) - j
    used = among(q, 0, 3) & among(r, 0, 3) & (lane < DENSE)
    base = jnp.where(used, (q * 3 + r) * 24 + (k >> 3) * 8, 1024)
    odd = ((k >> 2) & 1) * 4 + (up & 1) * 2 + (along & 1)
    band = lax.broadcasted_iota(jnp.int32, (512, 216), 1) - base
    flips = band & odd
    sign = jnp.where(((flips ^ (flips >> 1) ^ (flips >> 2)) & 1) == 1, -1.0, 1.0)
    return jnp.where(among(band, 0, 8), sign, 0.0).astype(BF16)


def merge_order():
    row = index(WIDTH)
    return one_hot((row & 127) * 4 + (row >> 7), WIDTH)


def turned(plan):
    row = index(plan.tokens)
    part = row // plan.group
    rest = row - part * plan.group
    return one_hot((rest >> 2) * SPAN + part * 4 + (rest & 3), plan.tokens)


def turned_back(plan):
    row = index(plan.frames * SPAN)
    target = ((row >> 2) & 3) * (plan.frames * 4) + (row >> 4) * 4 + (row & 3)
    return one_hot(target, plan.frames * SPAN)


def frame_of(plan, start, step):
    return (start + plan.times + step) & (plan.times - 1)


def window_of(plan, start):
    row = index(plan.frames * SPAN)
    return one_hot(frame_of(plan, start, row >> 4) * SPAN + (row & 15), plan.tokens)


def window_turned(plan, start):
    row = index(plan.frames * SPAN)
    part = row // (plan.frames * 4)
    rest = row - part * plan.frames * 4
    frame = frame_of(plan, start, rest >> 2)
    return one_hot(frame * SPAN + part * 4 + (rest & 3), plan.tokens)


def dot(a, b):
    return jnp.dot(a, b, preferred_element_type=jnp.float32)


def dot_t(a, b):
    return lax.dot_general(a, b, (((1,), (1,)), ((), ())), preferred_element_type=jnp.float32)


def kernel(
    plan, counts,
    video_in, w_conv_in, w_merge_in, w_qkv_in, w_out_in,
    out,
    video, w_conv, w_merge, w_qkv, w_out,
    rows_out, rows_in, cols_out, cols_in, corners_out, corners_in,
    parts_out, parts_in,
    patches, taps, merge, latent, normed, queries, pairs, mixed, encoded, turn, back,
    loaded, rows_sent, rows_got, cols_sent, cols_got, corners_sent, corners_got,
    parts_sent, parts_got, out_sent, out_got, own_done,
):
    ring = plan.ring
    me, high, side = lax.axis_index("tm"), lax.axis_index("height"), lax.axis_index("width")
    highs, sides = counts
    above, below = lax.rem(high + highs - 1, highs), lax.rem(high + 1, highs)
    before, after = lax.rem(side + sides - 1, sides), lax.rem(side + 1, sides)

    loads = [
        pltpu.make_async_copy(source, target, loaded.at[n])
        for n, (source, target) in enumerate(
            (
                (video_in, video), (w_conv_in, w_conv), (w_merge_in, w_merge),
                (w_qkv_in, w_qkv), (w_out_in, w_out),
            )
        )
    ]
    loads[0].start()

    barrier = pltpu.get_barrier_semaphore()
    beside = [{"height": peer} for peer in (above, below)]
    beside += [{"width": peer} for peer in (before, after)]
    beside += [{"height": u, "width": v} for u in (above, below) for v in (before, after)]
    for peer in beside:
        pl.semaphore_signal(barrier, inc=1, device_id=peer, device_id_type=MESH)

    def greet(k, _):
        peer = lax.rem(me + k, ring)
        pl.semaphore_signal(barrier, inc=1, device_id={"tm": peer}, device_id_type=MESH)
        return 0

    lax.fori_loop(1, ring, greet, 0)
    for load in loads[1:]:
        load.start()

    strip, edge = strip_rows(), edge_columns()
    unit_main, unit_halo = unit_rows()
    block_main, block_halo = block_columns()
    loads[0].wait()
    pixels = video[...].reshape(CHANS * FRAMES * ROWS, COLS)
    strips = dot(strip, pixels).astype(BF16)
    rows_out[0] = strips[:32]
    rows_out[1] = strips[32:64]
    edges = dot_t(edge, pixels).astype(BF16)
    cols_out[0] = edges[:16]
    cols_out[1] = edges[16:]
    corners = dot_t(edge, strips).astype(BF16)
    corners_out[0] = corners[:16]
    corners_out[1] = corners[16:]
    pl.semaphore_wait(barrier, ring - 1 + len(beside))

    def border_copy(source, target, sent, got, at, into, peer):
        return pltpu.make_async_remote_copy(
            src_ref=source.at[at], dst_ref=target.at[into], send_sem=sent.at[into],
            recv_sem=got.at[into], device_id=peer, device_id_type=MESH,
        )

    border_copies = []
    for down, u in enumerate((below, above)):
        border_copies.append(
            border_copy(rows_out, rows_in, rows_sent, rows_got, down, down, {"height": u})
        )
    for along, v in enumerate((after, before)):
        border_copies.append(
            border_copy(cols_out, cols_in, cols_sent, cols_got, along, along, {"width": v})
        )
    for down, u in enumerate((below, above)):
        for along, v in enumerate((after, before)):
            border_copies.append(
                border_copy(
                    corners_out, corners_in, corners_sent, corners_got, along, down * 2 + along,
                    {"height": u, "width": v},
                )
            )
    for copy in border_copies:
        copy.start()
    inner = dot(unit_main, pixels)
    lanes = unit_lanes()
    place, spare = part_rows(plan), spare_lanes()
    for copy in border_copies:
        copy.wait()

    def kept(value, condition):
        return jnp.where(condition, value, jnp.zeros_like(value))

    has_rows, has_cols = (high > 0, high < highs - 1), (side > 0, side < sides - 1)
    halo = [kept(rows_in[n], has_rows[n]) for n in range(2)]
    halo = jnp.concatenate(halo + [jnp.zeros((64, COLS), BF16)], axis=0)
    units = (inner + dot(unit_halo, halo)).astype(BF16)
    cols = jnp.concatenate([kept(cols_in[n], has_cols[n]) for n in range(2)], axis=0)
    strip_lane = lax.broadcasted_iota(jnp.int32, (16, 128), 1)
    corner = jnp.concatenate(
        [
            jnp.where(
                strip_lane < 32,
                kept(corners_in[n], has_rows[0] & has_cols[n]),
                kept(corners_in[2 + n], has_rows[1] & has_cols[n]),
            )
            for n in range(2)
        ],
        axis=0,
    )
    sidelong = (dot_t(cols, unit_main) + dot_t(corner, unit_halo)).astype(BF16)
    spread = (dot_t(block_main, units) + dot(block_halo, sidelong)).astype(BF16)

    stacked = jnp.concatenate(
        [
            jnp.concatenate(
                [spread[c * STEPS : (c + 1) * STEPS, q * 128 : (q + 1) * 128] for c in range(4)], axis=1
            )
            for q in range(UNITS // 4)
        ],
        axis=0,
    )
    stacked = dot(stacked, lanes).astype(BF16)

    def piece(t, up, jx):
        q, u = divmod(t * (TALL + 1) + up, 4)
        start = q * STEPS + jx * SPAN
        return stacked[start : start + 32, u * 128 : (u + 1) * 128]

    def pack(part):
        every = []
        for block in range(plan.blocks):
            jy, jx = divmod(block, ACROSS)
            pieces = []
            for unit in range(part * plan.units, (part + 1) * plan.units):
                up, t = divmod(unit, TIMES)
                pieces.append(piece(t, jy * plan.tall + up, jx))
            every.append(jnp.concatenate(pieces, axis=0))
        placed = dot(place, jnp.concatenate(every, axis=1)).astype(BF16)
        placed = [
            jnp.concatenate(
                [
                    placed[n * LINES : (n + 1) * LINES, block * 128 : (block + 1) * 128]
                    for n in range(4)
                ],
                axis=1,
            )
            for block in range(plan.blocks)
        ]
        return dot(jnp.concatenate(placed, axis=0), spare).astype(BF16)

    stages = ((0, 0, LINES), (1, 0, AHEAD), (1, AHEAD, LINES - AHEAD))

    def part_copy(stage, source, target):
        part, start, count = stages[stage]
        return pltpu.make_async_remote_copy(
            src_ref=parts_out.at[part, lax.rem(target, plan.blocks), pl.ds(start, count)],
            dst_ref=parts_in.at[part, source, pl.ds(start, count)],
            send_sem=parts_sent.at[stage, target], recv_sem=parts_got.at[stage, source],
            device_id={"tm": target}, device_id_type=MESH,
        )

    def ahead_by(k):
        step = ring - k
        ahead = (step + 1) // 2
        return lax.select(lax.rem(step, 2) == 1, ahead, ring - ahead)

    def send_parts(stage):
        def send(k, _):
            part_copy(stage, me, lax.rem(me + ahead_by(k), ring)).start()
            return 0

        lax.fori_loop(1, ring, send, 0)

    for part in range(PARTS):
        packed = pack(part)
        for block in range(plan.blocks):
            parts_out[part, block] = packed[block * LINES : (block + 1) * LINES]
        for stage in ((0,), (1, 2))[part]:
            send_parts(stage)
        parts_in[part, me] = parts_out[part, lax.rem(me, plan.blocks)]

    loads[1].wait()
    for out_pixel in range(4):
        signs = tap_signs(out_pixel)
        for dt in range(3):
            taps[dt * WIDTH : (dt + 1) * WIDTH, out_pixel * 128 : (out_pixel + 1) * 128] = (
                dot(signs, w_conv[dt]) * (1.0 / math.sqrt(8.0))
            ).astype(BF16)
    loads[2].wait()
    merge[...] = dot(merge_order(), w_merge[...]).astype(BF16)
    turn[...] = turned(plan)
    back[...] = turned_back(plan)
    for y in range(plan.tall):
        patches[y, 0 : 2 * SPAN, :] = jnp.zeros((2 * SPAN, WIDTH), BF16)
    loads[3].wait()
    loads[4].wait()

    apart = part_lanes()

    def take(stage):
        part, start, count = stages[stage]
        lines = start + count
        first, units = ((0, plan.units), (0, 1), (1, plan.units - 1))[stage]
        batch = (4, 16, 8)[stage]
        pick = window_rows(first, units, lines)

        def one(k, _):
            sources = []
            for n in range(batch):
                at = k * batch + n + 1
                source = lax.rem(me + ahead_by(at), ring)
                sources.append(source)

                @pl.when(at < ring)
                def _():
                    part_copy(stage, source, me).wait_recv()

            rows = jnp.concatenate([parts_in[part, source, :lines] for source in sources], axis=0)
            rows = dot(rows, apart).astype(BF16)
            rows = jnp.concatenate(
                [
                    jnp.concatenate(
                        [
                            rows[n * lines : (n + 1) * lines, copy * 128 : (copy + 1) * 128]
                            for copy in range(4)
                        ],
                        axis=0,
                    )
                    for n in range(batch)
                ],
                axis=1,
            )
            windows = dot(pick, rows).astype(BF16)
            for n, source in enumerate(sources):
                for unit in range(units):
                    up, t = divmod(part * plan.units + first + unit, TIMES)
                    at = pl.multiple_of((source * TIMES + t + 2) * SPAN, SPAN)
                    for dx in range(2):
                        row = unit * 32 + dx * SPAN
                        value = windows[row : row + SPAN, n * 128 : (n + 1) * 128]
                        for dy in range(2):
                            if 0 <= up - dy < plan.tall:
                                tap = dy * 2 + dx
                                patches[
                                    up - dy, pl.ds(at, SPAN), tap * 128 : (tap + 1) * 128
                                ] = value
            return 0

        lax.fori_loop(0, ring // batch, one, 0)

    half = plan.tokens // 2
    group = plan.group
    lane = lax.broadcasted_iota(jnp.int32, (1, 128), 1)
    head_scale = [
        jnp.where((lane < 64) == (head == 0), 0.125, 0.0).astype(BF16) for head in range(2)
    ]
    ones = jnp.ones((group, 128), BF16)
    some = plan.frames * 4
    query_at = lax.broadcasted_iota(jnp.int32, (2 * some, group), 0) & (some - 1)
    key_at = lax.broadcasted_iota(jnp.int32, (2 * some, group), 1)
    same = (query_at & 3) == (key_at & 3)

    far = ring // 4
    start = (me - far) * TIMES + 1
    queries_turned, window = window_turned(plan, start), window_of(plan, start)
    allowed = same & (frame_of(plan, start, query_at >> 2) >= (key_at >> 2))

    def place_of(source, y, first, count):
        block = lax.rem(source, plan.blocks)
        line = (block // ACROSS) * plan.tall + y
        column = pl.multiple_of(lax.rem(block, ACROSS) * SPAN, SPAN)
        return out.at[pl.ds(first, count), line, pl.ds(column, SPAN), :]

    def out_copies(y, source_of):
        copies = []
        for slot, ahead in enumerate(reach):
            source = source_of(ahead)
            first, count = (0, 1) if ahead == far else (1, 1) if ahead == -far else (0, TIMES)
            at = max(0, (ahead + far) * TIMES - 1)
            copies.append(
                pltpu.make_async_remote_copy(
                    src_ref=encoded.at[y, pl.ds(at, count)],
                    dst_ref=place_of(source, y, first, count),
                    send_sem=out_sent.at[y, slot], recv_sem=out_got.at[y, slot],
                    device_id={"tm": lax.rem(source + ahead + ring, ring)}, device_id_type=MESH,
                )
            )
        return copies

    reach = [way * ahead for ahead in range(far, 0, -1) for way in (1, -1)]

    def own_copy(y):
        return pltpu.make_async_copy(
            encoded.at[y, pl.ds(far * TIMES - 1, TIMES)], place_of(me, y, 0, TIMES), own_done.at[y]
        )

    def one_row(y, _):
        for stage in range(len(stages)):
            pl.when(y == stage)(functools.partial(take, stage))

        for m in range(2):
            at = m * half
            around = [patches[y, at + dt * SPAN : at + dt * SPAN + half, :] for dt in range(3)]
            total = 0.5 * dot(jnp.concatenate(around, axis=1), taps[...])
            active = (total + total * jnp.tanh(total)).astype(BF16)
            value = dot(active, merge[...]).astype(BF16)
            latent[at : at + half, :] = value
            wide = value.astype(jnp.float32)
            meansq = jnp.mean(wide * wide, axis=-1, keepdims=True)
            normed[at : at + half, :] = (wide * lax.rsqrt(meansq + 1e-06)).astype(BF16)

        tokens = dot(queries_turned, normed[...]).astype(BF16)
        queries[...] = dot(tokens, w_qkv[:, :WIDTH]).astype(BF16)
        tokens = dot(turn[...], normed[...]).astype(BF16)
        for part in range(2):
            columns = slice(part * WIDTH, (part + 1) * WIDTH)
            pairs[:, columns] = dot(
                tokens, w_qkv[:, (part + 1) * WIDTH : (part + 2) * WIDTH]
            ).astype(BF16)

        for part in range(SPAN // 4):
            asked = slice(part * some, (part + 1) * some)
            rows = slice(part * group, (part + 1) * group)
            for pair in range(HEADS // 2):
                columns = slice(pair * 128, (pair + 1) * 128)
                query, keys = queries[asked, columns], pairs[rows, columns]
                values = pairs[rows, WIDTH + pair * 128 : WIDTH + (pair + 1) * 128]
                both = jnp.concatenate([query * head_scale[0], query * head_scale[1]], axis=0)
                scores = jnp.where(allowed, dot_t(both, keys), -1e30)
                expon = jnp.exp(scores - jnp.max(scores, axis=-1, keepdims=True)).astype(BF16)
                total = dot(expon, jnp.concatenate([values, ones], axis=1))
                result = total[:, :128] / total[:, 128:]
                mixed[asked, columns] = jnp.where(lane < 64, result[:some], result[some:]).astype(BF16)

        straight = dot(back[...], mixed[...]).astype(BF16)
        total = dot(straight, w_out[...]) + dot(window, latent[...])
        encoded[y] = total.astype(BF16).reshape(plan.frames, SPAN, WIDTH)

        for copy in out_copies(y, lambda ahead: me):
            copy.start()
        own_copy(y).start()
        return 0

    lax.fori_loop(0, plan.tall, one_row, 0)

    def parts_left(k, _):
        for stage in range(len(stages)):
            part_copy(stage, me, lax.rem(me + ahead_by(k), ring)).wait_send()
        return 0

    lax.fori_loop(1, ring, parts_left, 0)

    def all_done(y, _):
        for copy in out_copies(y, lambda ahead: me):
            copy.wait_send()
        for copy in out_copies(y, lambda ahead: lax.rem(me - ahead + ring, ring)):
            copy.wait_recv()
        own_copy(y).wait()
        return 0

    lax.fori_loop(0, plan.tall, all_done, 0)


def copied(value):
    def body(source, target, done):
        rows = value.shape[1]
        copies = []
        for n in range(COPIES):
            at = (n // (COPIES // 2), pl.ds(n % (COPIES // 2) * (rows // (COPIES // 2)), rows // (COPIES // 2)))
            copies.append(pltpu.make_async_copy(source.at[at], target.at[at], done.at[n]))
        for copy in copies:
            copy.start()
        for copy in copies:
            copy.wait()

    return pl.pallas_call(
        body,
        out_shape=jax.ShapeDtypeStruct(value.shape, value.dtype),
        in_specs=[pl.BlockSpec(memory_space=pltpu.VMEM)],
        out_specs=pl.BlockSpec(memory_space=pl.ANY),
        scratch_shapes=[pltpu.SemaphoreType.DMA((COPIES,))],
        compiler_params=pltpu.CompilerParams(vmem_limit_bytes=2**20),
    )(value)


def solution(mesh):
    plan = Plan(mesh.shape["tm"])
    counts = (mesh.shape["height"], mesh.shape["width"])

    def shards(video, w_conv, w_merge, w_qkv, w_out):
        operands = (video, w_conv.reshape(3, 216, 128), w_merge, w_qkv, w_out)
        dma = pltpu.SemaphoreType.DMA
        held = [pltpu.VMEM(one.shape, BF16) for one in operands]
        buffers = [
            (2, 32, COLS), (2, 32, COLS),
            (2, 16, CHANS * FRAMES * ROWS), (2, 16, CHANS * FRAMES * ROWS),
            (2, 16, 128), (4, 16, 128),
            (PARTS, plan.blocks, LINES, 128), (PARTS, plan.ring, LINES, 128),
            (plan.tall, plan.tokens + 2 * SPAN, WIDTH),
            (3 * WIDTH, WIDTH), (WIDTH, WIDTH),
            (plan.tokens, WIDTH), (plan.tokens, WIDTH),
            (plan.frames * SPAN, WIDTH), (plan.tokens, 2 * WIDTH), (plan.frames * SPAN, WIDTH),
            (plan.tall, plan.frames, SPAN, WIDTH),
            (plan.tokens, plan.tokens), (plan.frames * SPAN, plan.frames * SPAN),
        ]
        semaphores = [
            (len(operands),), (2,), (2,), (2,), (2,), (4,), (4,),
            (PARTS + 1, plan.ring), (PARTS + 1, plan.ring),
            (plan.tall, plan.ring // 2), (plan.tall, plan.ring // 2), (plan.tall,),
        ]
        return copied(pl.pallas_call(
            functools.partial(kernel, plan, counts),
            out_shape=pltpu.VMEM((TIMES, TALL, WIDE, WIDTH), BF16),
            in_specs=[pl.BlockSpec(memory_space=pltpu.HBM)] * len(operands),
            out_specs=pl.BlockSpec(memory_space=pl.ANY),
            scratch_shapes=held
            + [pltpu.VMEM(shape, BF16) for shape in buffers]
            + [dma(shape) for shape in semaphores],
            compiler_params=pltpu.CompilerParams(
                collective_id=0, has_side_effects=True, vmem_limit_bytes=56 * 2**20
            ),
            cost_estimate=pl.CostEstimate(
                flops=8 * 10**9, bytes_accessed=6 * 10**6, transcendentals=2 * 10**6
            ),
        )(*operands))

    return jax.shard_map(
        shards,
        mesh=mesh,
        in_specs=(P(None, "tm", "height", "width"), P(), P(), P(), P()),
        out_specs=P("tm", "height", "width", None),
        check_vma=False,
    )
```

```python
import functools
import math

import jax
import jax.numpy as jnp
from jax import lax
from jax.experimental import pallas as pl
from jax.experimental.pallas import tpu as pltpu
from jax.sharding import PartitionSpec as P

HEADS = 8

CHANS, FRAMES, ROWS, COLS = 3, 4, 32, 256
TIMES = FRAMES // 2
BLOCK = 4
TALL, WIDE = ROWS // BLOCK, COLS // BLOCK
SPAN = 16
ACROSS = WIDE // SPAN
UNIT = 32
STEPS = 80
UNITS = 20
WIDTH = 512
PARTS = 2
LINES = 64
AHEAD = 16
COPIES = 8
EARLY = (5, 6)
DENSE = 96
SPARE = 32
BF16 = jnp.bfloat16
MESH = pl.DeviceIdType.MESH


class Plan:
    def __init__(self, ring):
        self.ring = ring
        self.times = ring * TIMES
        self.blocks = ring // 2
        self.tall = TALL * ACROSS // self.blocks
        self.units = TIMES * (self.tall + 1) // PARTS
        self.tokens = self.times * SPAN
        self.group = self.times * 4
        self.frames = self.times // 2


def index(count):
    return lax.broadcasted_iota(jnp.int32, (count, 1), 0)


def among(value, low, high):
    return (value >= low) & (value < high)


def one_hot(target, width):
    lane = lax.broadcasted_iota(jnp.int32, (target.shape[0], width), 1)
    return jnp.where(lane == target, 1.0, 0.0).astype(BF16)


def strip_rows():
    row = index(128)
    side, rest = row >> 5, row & 31
    target = (rest >> 1) * ROWS + (1 - side) * (ROWS - 2) + (rest & 1)
    used = (rest < 2 * CHANS * FRAMES) & (side < 2)
    return one_hot(jnp.where(used, target, -1), CHANS * FRAMES * ROWS)


def unit_rows():
    row = index(UNITS * UNIT)
    unit, k = row >> 5, row & 31
    late = jnp.where(unit >= TALL + 1, 1, 0)
    plane = (k >> 3) * FRAMES + 2 * late + ((k >> 2) & 1)
    at = (unit - late * (TALL + 1)) * BLOCK + (k & 3) - 2
    used = (unit < 2 * (TALL + 1)) & (k < 24)
    main = jnp.where(used & among(at, 0, ROWS), plane * ROWS + at, -1)
    halo = jnp.where(at < 0, plane * 2 + at + 2, 32 + plane * 2 + at - ROWS)
    halo = jnp.where(used & ~among(at, 0, ROWS), halo, -1)
    return one_hot(main, CHANS * FRAMES * ROWS), one_hot(halo, 128)


def edge_columns():
    row = index(32)
    line = row & 15
    return one_hot(jnp.where(line < 2, line + (1 - (row >> 4)) * (COLS - 2), -1), COLS)


def block_columns():
    row = index(BLOCK * STEPS)
    c = sum(jnp.where(row >= n * STEPS, 1, 0) for n in range(1, BLOCK))
    x = row - c * STEPS
    at = x * BLOCK + c - 2
    main = jnp.where(among(at, 0, COLS), at, -1)
    halo = jnp.where(at < 0, at + 2, jnp.where(x <= WIDE, 16 + at - COLS, -1))
    return one_hot(main, COLS), one_hot(jnp.where(among(at, 0, COLS), -1, halo), 32)


def unit_lanes():
    row = index(512)
    k = row & 31
    target = ((row >> 5) & 3) * 128 + (row >> 7) * 24 + k
    return one_hot(jnp.where(k < 24, target, -1), 512)


def part_rows(plan):
    row = index(LINES)
    late = jnp.where(row >= AHEAD, 1, 0)
    below = row - late * AHEAD
    third = (below * 171) >> 9
    piece = below - 3 * third

    def source(item):
        unit = (item * 3856) >> 16
        return unit * 32 + item - unit * (SPAN + 1)

    width = plan.units * 32
    every = [one_hot(source(row + 5 * late), width)]
    used = (late == 1) | (below < 15)
    for n in range(3):
        item = jnp.where(late == 1, 69, 16) + third
        every.append(one_hot(jnp.where(used & (piece == n), source(item), -1), width))
    return jnp.concatenate(every, axis=0)


def spare_lanes():
    lane = index(128)
    every = [one_hot(jnp.where(lane < DENSE, lane, -1), 128)]
    for piece in range(3):
        at = lane - piece * SPARE
        every.append(one_hot(jnp.where(among(at, 0, SPARE), DENSE + at, -1), 128))
    return jnp.concatenate(every, axis=0)


def part_lanes():
    lane = index(128)
    every = [one_hot(jnp.where(lane < DENSE, lane, -1), 128)]
    for piece in range(3):
        every.append(one_hot(jnp.where(lane >= DENSE, lane - DENSE + piece * SPARE, -1), 128))
    return jnp.concatenate(every, axis=1)


def window_rows(first, units, lines):
    row = index(units * 32)
    item = (first + (row >> 5)) * (SPAN + 1) + (row & 15) + ((row >> 4) & 1)
    main = jnp.where(item < 16, item, jnp.where(among(item, 21, 69), item - 5, -1))
    total = one_hot(main, 4 * lines)
    rest = jnp.where(item < 69, 3 * (item - 16), AHEAD + 3 * (item - 69))
    for piece in range(3):
        at = (1 + piece) * lines + rest + piece
        total += one_hot(jnp.where(main < 0, at, -1), 4 * lines)
    return total


def tap_signs(out_pixel):
    i, j = divmod(out_pixel, 2)
    row = index(512)
    lane = row & 127
    c = sum(jnp.where(lane >= n * 24, 1, 0) for n in range(1, BLOCK))
    k = lane - c * 24
    up, along = ((row >> 8) & 1) * 4 + (k & 3), ((row >> 7) & 1) * 4 + c
    q, r = (up >> 1) - i, (along >> 1) - j
    used = among(q, 0, 3) & among(r, 0, 3) & (lane < DENSE)
    base = jnp.where(used, (q * 3 + r) * 24 + (k >> 3) * 8, 1024)
    odd = ((k >> 2) & 1) * 4 + (up & 1) * 2 + (along & 1)
    band = lax.broadcasted_iota(jnp.int32, (512, 216), 1) - base
    flips = band & odd
    sign = jnp.where(((flips ^ (flips >> 1) ^ (flips >> 2)) & 1) == 1, -1.0, 1.0)
    return jnp.where(among(band, 0, 8), sign, 0.0).astype(BF16)


def merge_order():
    row = index(WIDTH)
    return one_hot((row & 127) * 4 + (row >> 7), WIDTH)


def turned(plan):
    row = index(plan.tokens)
    part = row // plan.group
    rest = row - part * plan.group
    return one_hot((rest >> 2) * SPAN + part * 4 + (rest & 3), plan.tokens)


def turned_back(plan):
    row = index(plan.frames * SPAN)
    target = ((row >> 2) & 3) * (plan.frames * 4) + (row >> 4) * 4 + (row & 3)
    return one_hot(target, plan.frames * SPAN)


def frame_of(plan, start, step):
    return (start + plan.times + step) & (plan.times - 1)


def window_of(plan, start):
    row = index(plan.frames * SPAN)
    return one_hot(frame_of(plan, start, row >> 4) * SPAN + (row & 15), plan.tokens)


def window_turned(plan, start):
    row = index(plan.frames * SPAN)
    part = row // (plan.frames * 4)
    rest = row - part * plan.frames * 4
    frame = frame_of(plan, start, rest >> 2)
    return one_hot(frame * SPAN + part * 4 + (rest & 3), plan.tokens)


def dot(a, b):
    return jnp.dot(a, b, preferred_element_type=jnp.float32)


def dot_t(a, b):
    return lax.dot_general(a, b, (((1,), (1,)), ((), ())), preferred_element_type=jnp.float32)


def kernel(
    plan, counts,
    video_in, w_conv_in, w_merge_in, w_qkv_in, w_out_in,
    out,
    video, w_conv, w_merge, w_qkv, w_out,
    rows_out, rows_in, cols_out, cols_in, corners_out, corners_in,
    parts_out, parts_in,
    patches, taps, merge, latent, normed, queries, pairs, mixed, encoded, turn, back,
    loaded, rows_sent, rows_got, cols_sent, cols_got, corners_sent, corners_got,
    parts_sent, parts_got, out_sent, out_got, own_done,
):
    ring = plan.ring
    me, high, side = lax.axis_index("tm"), lax.axis_index("height"), lax.axis_index("width")
    highs, sides = counts
    above, below = lax.rem(high + highs - 1, highs), lax.rem(high + 1, highs)
    before, after = lax.rem(side + sides - 1, sides), lax.rem(side + 1, sides)

    loads = [
        pltpu.make_async_copy(source, target, loaded.at[n])
        for n, (source, target) in enumerate(
            (
                (video_in, video), (w_conv_in, w_conv), (w_merge_in, w_merge),
                (w_qkv_in, w_qkv), (w_out_in, w_out),
            )
        )
    ]
    loads[0].start()

    barrier = pltpu.get_barrier_semaphore()
    beside = [{"height": peer} for peer in (above, below)]
    beside += [{"width": peer} for peer in (before, after)]
    beside += [{"height": u, "width": v} for u in (above, below) for v in (before, after)]
    for peer in beside:
        pl.semaphore_signal(barrier, inc=1, device_id=peer, device_id_type=MESH)

    def greet(k, _):
        peer = lax.rem(me + k, ring)
        pl.semaphore_signal(barrier, inc=1, device_id={"tm": peer}, device_id_type=MESH)
        return 0

    lax.fori_loop(1, ring, greet, 0)
    for load in loads[1:]:
        load.start()

    strip, edge = strip_rows(), edge_columns()
    unit_main, unit_halo = unit_rows()
    block_main, block_halo = block_columns()
    loads[0].wait()
    pixels = video[...].reshape(CHANS * FRAMES * ROWS, COLS)
    strips = dot(strip, pixels).astype(BF16)
    rows_out[0] = strips[:32]
    rows_out[1] = strips[32:64]
    edges = dot_t(edge, pixels).astype(BF16)
    cols_out[0] = edges[:16]
    cols_out[1] = edges[16:]
    corners = dot_t(edge, strips).astype(BF16)
    corners_out[0] = corners[:16]
    corners_out[1] = corners[16:]
    pl.semaphore_wait(barrier, ring - 1 + len(beside))

    def border_copy(source, target, sent, got, at, into, peer):
        return pltpu.make_async_remote_copy(
            src_ref=source.at[at], dst_ref=target.at[into], send_sem=sent.at[into],
            recv_sem=got.at[into], device_id=peer, device_id_type=MESH,
        )

    border_copies = []
    for down, u in enumerate((below, above)):
        border_copies.append(
            border_copy(rows_out, rows_in, rows_sent, rows_got, down, down, {"height": u})
        )
    for along, v in enumerate((after, before)):
        border_copies.append(
            border_copy(cols_out, cols_in, cols_sent, cols_got, along, along, {"width": v})
        )
    for down, u in enumerate((below, above)):
        for along, v in enumerate((after, before)):
            border_copies.append(
                border_copy(
                    corners_out, corners_in, corners_sent, corners_got, along, down * 2 + along,
                    {"height": u, "width": v},
                )
            )
    for copy in border_copies:
        copy.start()
    inner = dot(unit_main, pixels)
    lanes = unit_lanes()
    place, spare = part_rows(plan), spare_lanes()

    def stack(spread):
        quads = [
            jnp.concatenate(
                [spread[c * STEPS : (c + 1) * STEPS, q * 128 : (q + 1) * 128] for c in range(4)], axis=1
            )
            for q in range(spread.shape[1] // 128)
        ]
        return dot(jnp.concatenate(quads, axis=0), lanes).astype(BF16)

    def pack(stacked, quads, part, blocks):
        every = []
        for block in blocks:
            jy, jx = divmod(block, ACROSS)
            pieces = []
            for unit in range(part * plan.units, (part + 1) * plan.units):
                up, t = divmod(unit, TIMES)
                q, u = divmod(t * (TALL + 1) + jy * plan.tall + up, 4)
                at = quads.index(q) * STEPS + jx * SPAN
                pieces.append(stacked[at : at + 32, u * 128 : (u + 1) * 128])
            every.append(jnp.concatenate(pieces, axis=0))
        placed = dot(place, jnp.concatenate(every, axis=1)).astype(BF16)
        placed = [
            jnp.concatenate(
                [placed[m * LINES : (m + 1) * LINES, n * 128 : (n + 1) * 128] for m in range(4)], axis=1
            )
            for n in range(len(blocks))
        ]
        packed = dot(jnp.concatenate(placed, axis=0), spare).astype(BF16)
        for n, block in enumerate(blocks):
            parts_out[part, block] = packed[n * LINES : (n + 1) * LINES]

    stages = ((0, 0, LINES), (1, 0, AHEAD), (1, AHEAD, LINES - AHEAD))

    def part_copy(stage, source, target):
        part, start, count = stages[stage]
        return pltpu.make_async_remote_copy(
            src_ref=parts_out.at[part, lax.rem(target, plan.blocks), pl.ds(start, count)],
            dst_ref=parts_in.at[part, source, pl.ds(start, count)],
            send_sem=parts_sent.at[stage, target], recv_sem=parts_got.at[stage, source],
            device_id={"tm": target}, device_id_type=MESH,
        )

    def ahead_by(k):
        step = ring - k
        ahead = (step + 1) // 2
        return lax.select(lax.rem(step, 2) == 1, ahead, ring - ahead)

    def send_parts(stage):
        def send(k, _):
            target = lax.rem(me + ahead_by(k), ring)

            @pl.when((stage > 0) | ~among(lax.rem(target, plan.blocks), EARLY[0], EARLY[-1] + 1))
            def _():
                part_copy(stage, me, target).start()

            return 0

        lax.fori_loop(1, ring, send, 0)

    quads = (1, 3)
    early = jnp.concatenate([inner[q * 128 : (q + 1) * 128] for q in quads], axis=0).astype(BF16)
    pack(stack(dot_t(block_main, early).astype(BF16)), quads, 0, EARLY)
    for target in range(ring):
        if target % plan.blocks in EARLY:

            @pl.when(me != target)
            def _():
                part_copy(0, me, target).start()

    for copy in border_copies:
        copy.wait()

    def kept(value, condition):
        return jnp.where(condition, value, jnp.zeros_like(value))

    has_rows, has_cols = (high > 0, high < highs - 1), (side > 0, side < sides - 1)
    halo = [kept(rows_in[n], has_rows[n]) for n in range(2)]
    halo = jnp.concatenate(halo + [jnp.zeros((64, COLS), BF16)], axis=0)
    units = (inner + dot(unit_halo, halo)).astype(BF16)
    cols = jnp.concatenate([kept(cols_in[n], has_cols[n]) for n in range(2)], axis=0)
    strip_lane = lax.broadcasted_iota(jnp.int32, (16, 128), 1)
    corner = jnp.concatenate(
        [
            jnp.where(
                strip_lane < 32,
                kept(corners_in[n], has_rows[0] & has_cols[n]),
                kept(corners_in[2 + n], has_rows[1] & has_cols[n]),
            )
            for n in range(2)
        ],
        axis=0,
    )
    sidelong = (dot_t(cols, unit_main) + dot_t(corner, unit_halo)).astype(BF16)
    spread = (dot_t(block_main, units) + dot(block_halo, sidelong)).astype(BF16)

    stacked, quads = stack(spread), tuple(range(UNITS // 4))
    pack(stacked, quads, 0, [block for block in range(plan.blocks) if block not in EARLY])
    send_parts(0)
    parts_in[0, me] = parts_out[0, lax.rem(me, plan.blocks)]
    pack(stacked, quads, 1, range(plan.blocks))
    send_parts(1)
    send_parts(2)
    parts_in[1, me] = parts_out[1, lax.rem(me, plan.blocks)]

    loads[1].wait()
    for out_pixel in range(4):
        signs = tap_signs(out_pixel)
        for dt in range(3):
            taps[dt * WIDTH : (dt + 1) * WIDTH, out_pixel * 128 : (out_pixel + 1) * 128] = (
                dot(signs, w_conv[dt]) * (1.0 / math.sqrt(8.0))
            ).astype(BF16)
    loads[2].wait()
    merge[...] = dot(merge_order(), w_merge[...]).astype(BF16)
    turn[: plan.tokens] = turned(plan)
    back[...] = turned_back(plan)
    for y in range(plan.tall):
        patches[y, 0 : 2 * SPAN, :] = jnp.zeros((2 * SPAN, WIDTH), BF16)
    loads[3].wait()
    loads[4].wait()

    apart = part_lanes()

    def take(stage):
        part, start, count = stages[stage]
        lines = start + count
        first, units = ((0, plan.units), (0, 1), (1, plan.units - 1))[stage]
        batch = (4, 16, 8)[stage]
        pick = window_rows(first, units, lines)

        def one(k, _):
            sources = []
            for n in range(batch):
                at = k * batch + n + 1
                source = lax.rem(me + ahead_by(at), ring)
                sources.append(source)

                @pl.when(at < ring)
                def _():
                    part_copy(stage, source, me).wait_recv()

            rows = jnp.concatenate([parts_in[part, source, :lines] for source in sources], axis=0)
            rows = dot(rows, apart).astype(BF16)
            rows = jnp.concatenate(
                [
                    jnp.concatenate(
                        [
                            rows[n * lines : (n + 1) * lines, copy * 128 : (copy + 1) * 128]
                            for copy in range(4)
                        ],
                        axis=0,
                    )
                    for n in range(batch)
                ],
                axis=1,
            )
            windows = dot(pick, rows).astype(BF16)
            for n, source in enumerate(sources):
                for unit in range(units):
                    up, t = divmod(part * plan.units + first + unit, TIMES)
                    at = pl.multiple_of((source * TIMES + t + 2) * SPAN, SPAN)
                    for dx in range(2):
                        row = unit * 32 + dx * SPAN
                        value = windows[row : row + SPAN, n * 128 : (n + 1) * 128]
                        for dy in range(2):
                            if 0 <= up - dy < plan.tall:
                                tap = dy * 2 + dx
                                patches[
                                    up - dy, pl.ds(at, SPAN), tap * 128 : (tap + 1) * 128
                                ] = value
            return 0

        lax.fori_loop(0, ring // batch, one, 0)

    half = plan.tokens // 2
    group = plan.group
    lane = lax.broadcasted_iota(jnp.int32, (1, 128), 1)
    head_scale = [
        jnp.where((lane < 64) == (head == 0), 0.125, 0.0).astype(BF16) for head in range(2)
    ]
    ones = jnp.ones((group, 128), BF16)
    some = plan.frames * 4
    query_at = lax.broadcasted_iota(jnp.int32, (2 * some, group), 0) & (some - 1)
    key_at = lax.broadcasted_iota(jnp.int32, (2 * some, group), 1)
    same = (query_at & 3) == (key_at & 3)

    far = ring // 4
    start = (me - far) * TIMES + 1
    turn[plan.tokens :] = window_turned(plan, start)
    window = window_of(plan, start)
    allowed = same & (frame_of(plan, start, query_at >> 2) >= (key_at >> 2))

    def place_of(source, y, first, count):
        block = lax.rem(source, plan.blocks)
        line = (block // ACROSS) * plan.tall + y
        column = pl.multiple_of(lax.rem(block, ACROSS) * SPAN, SPAN)
        return out.at[pl.ds(first, count), line, pl.ds(column, SPAN), :]

    def out_copies(y, source_of):
        copies = []
        for slot, ahead in enumerate(reach):
            source = source_of(ahead)
            first, count = (0, 1) if ahead == far else (1, 1) if ahead == -far else (0, TIMES)
            at = max(0, (ahead + far) * TIMES - 1)
            copies.append(
                pltpu.make_async_remote_copy(
                    src_ref=encoded.at[y, pl.ds(at, count)],
                    dst_ref=place_of(source, y, first, count),
                    send_sem=out_sent.at[y, slot], recv_sem=out_got.at[y, slot],
                    device_id={"tm": lax.rem(source + ahead + ring, ring)}, device_id_type=MESH,
                )
            )
        return copies

    reach = [way * ahead for ahead in range(far, 0, -1) for way in (1, -1)]

    def own_copy(y):
        return pltpu.make_async_copy(
            encoded.at[y, pl.ds(far * TIMES - 1, TIMES)], place_of(me, y, 0, TIMES), own_done.at[y]
        )

    def one_row(y, _):
        for stage in range(len(stages)):
            pl.when(y == stage)(functools.partial(take, stage))

        for m in range(2):
            at = m * half
            around = [patches[y, at + dt * SPAN : at + dt * SPAN + half, :] for dt in range(3)]
            total = 0.5 * dot(jnp.concatenate(around, axis=1), taps[...])
            active = (total + total * jnp.tanh(total)).astype(BF16)
            value = dot(active, merge[...]).astype(BF16)
            latent[at : at + half, :] = value
            wide = value.astype(jnp.float32)
            meansq = jnp.mean(wide * wide, axis=-1, keepdims=True)
            normed[at : at + half, :] = (wide * lax.rsqrt(meansq + 1e-06)).astype(BF16)

        tokens = dot(turn[...], normed[...]).astype(BF16)
        queries[...] = dot(tokens[plan.tokens :], w_qkv[:, :WIDTH]).astype(BF16)
        tokens = tokens[: plan.tokens]
        for part in range(2):
            columns = slice(part * WIDTH, (part + 1) * WIDTH)
            pairs[:, columns] = dot(
                tokens, w_qkv[:, (part + 1) * WIDTH : (part + 2) * WIDTH]
            ).astype(BF16)

        for part in range(SPAN // 4):
            asked = slice(part * some, (part + 1) * some)
            rows = slice(part * group, (part + 1) * group)
            for pair in range(HEADS // 2):
                columns = slice(pair * 128, (pair + 1) * 128)
                query, keys = queries[asked, columns], pairs[rows, columns]
                values = pairs[rows, WIDTH + pair * 128 : WIDTH + (pair + 1) * 128]
                both = jnp.concatenate([query * head_scale[0], query * head_scale[1]], axis=0)
                scores = jnp.where(allowed, dot_t(both, keys), -1e30)
                expon = jnp.exp(scores - jnp.max(scores, axis=-1, keepdims=True)).astype(BF16)
                total = dot(expon, jnp.concatenate([values, ones], axis=1))
                result = total[:, :128] / total[:, 128:]
                mixed[asked, columns] = jnp.where(lane < 64, result[:some], result[some:]).astype(BF16)

        straight = dot(back[...], mixed[...]).astype(BF16)
        total = dot(straight, w_out[...]) + dot(window, latent[...])
        encoded[y] = total.astype(BF16).reshape(plan.frames, SPAN, WIDTH)

        for copy in out_copies(y, lambda ahead: me):
            copy.start()
        own_copy(y).start()
        return 0

    lax.fori_loop(0, plan.tall, one_row, 0)

    def parts_left(k, _):
        for stage in range(len(stages)):
            part_copy(stage, me, lax.rem(me + ahead_by(k), ring)).wait_send()
        return 0

    lax.fori_loop(1, ring, parts_left, 0)

    def all_done(y, _):
        for copy in out_copies(y, lambda ahead: me):
            copy.wait_send()
        for copy in out_copies(y, lambda ahead: lax.rem(me - ahead + ring, ring)):
            copy.wait_recv()
        own_copy(y).wait()
        return 0

    lax.fori_loop(0, plan.tall, all_done, 0)


def copied(value):
    def body(source, target, done):
        rows = value.shape[1]
        copies = []
        for n in range(COPIES):
            at = (n // (COPIES // 2), pl.ds(n % (COPIES // 2) * (rows // (COPIES // 2)), rows // (COPIES // 2)))
            copies.append(pltpu.make_async_copy(source.at[at], target.at[at], done.at[n]))
        for copy in copies:
            copy.start()
        for copy in copies:
            copy.wait()

    return pl.pallas_call(
        body,
        out_shape=jax.ShapeDtypeStruct(value.shape, value.dtype),
        in_specs=[pl.BlockSpec(memory_space=pltpu.VMEM)],
        out_specs=pl.BlockSpec(memory_space=pl.ANY),
        scratch_shapes=[pltpu.SemaphoreType.DMA((COPIES,))],
        compiler_params=pltpu.CompilerParams(vmem_limit_bytes=2**20),
    )(value)


def solution(mesh):
    plan = Plan(mesh.shape["tm"])
    counts = (mesh.shape["height"], mesh.shape["width"])

    def shards(video, w_conv, w_merge, w_qkv, w_out):
        operands = (video, w_conv.reshape(3, 216, 128), w_merge, w_qkv, w_out)
        dma = pltpu.SemaphoreType.DMA
        held = [pltpu.VMEM(one.shape, BF16) for one in operands]
        buffers = [
            (2, 32, COLS), (2, 32, COLS),
            (2, 16, CHANS * FRAMES * ROWS), (2, 16, CHANS * FRAMES * ROWS),
            (2, 16, 128), (4, 16, 128),
            (PARTS, plan.blocks, LINES, 128), (PARTS, plan.ring, LINES, 128),
            (plan.tall, plan.tokens + 2 * SPAN, WIDTH),
            (3 * WIDTH, WIDTH), (WIDTH, WIDTH),
            (plan.tokens, WIDTH), (plan.tokens, WIDTH),
            (plan.frames * SPAN, WIDTH), (plan.tokens, 2 * WIDTH), (plan.frames * SPAN, WIDTH),
            (plan.tall, plan.frames, SPAN, WIDTH),
            (plan.tokens + plan.frames * SPAN, plan.tokens), (plan.frames * SPAN, plan.frames * SPAN),
        ]
        semaphores = [
            (len(operands),), (2,), (2,), (2,), (2,), (4,), (4,),
            (PARTS + 1, plan.ring), (PARTS + 1, plan.ring),
            (plan.tall, plan.ring // 2), (plan.tall, plan.ring // 2), (plan.tall,),
        ]
        return copied(pl.pallas_call(
            functools.partial(kernel, plan, counts),
            out_shape=pltpu.VMEM((TIMES, TALL, WIDE, WIDTH), BF16),
            in_specs=[pl.BlockSpec(memory_space=pltpu.HBM)] * len(operands),
            out_specs=pl.BlockSpec(memory_space=pl.ANY),
            scratch_shapes=held
            + [pltpu.VMEM(shape, BF16) for shape in buffers]
            + [dma(shape) for shape in semaphores],
            compiler_params=pltpu.CompilerParams(
                collective_id=0, has_side_effects=True, vmem_limit_bytes=56 * 2**20
            ),
            cost_estimate=pl.CostEstimate(
                flops=8 * 10**9, bytes_accessed=6 * 10**6, transcendentals=2 * 10**6
            ),
        )(*operands))

    return jax.shard_map(
        shards,
        mesh=mesh,
        in_specs=(P(None, "tm", "height", "width"), P(), P(), P(), P()),
        out_specs=P("tm", "height", "width", None),
        check_vma=False,
    )
```

```python
import functools
import math

import jax
import jax.numpy as jnp
from jax import lax
from jax.experimental import pallas as pl
from jax.experimental.pallas import tpu as pltpu
from jax.sharding import PartitionSpec as P

HEADS = 8

CHANS, FRAMES, ROWS, COLS = 3, 4, 32, 256
TIMES = FRAMES // 2
BLOCK = 4
TALL, WIDE = ROWS // BLOCK, COLS // BLOCK
SPAN = 16
ACROSS = WIDE // SPAN
UNIT = 32
STEPS = 80
UNITS = 20
WIDTH = 512
PARTS = 2
LINES = 64
AHEAD = 16
COPIES = 8
DENSE = 96
SPARE = 32
BF16 = jnp.bfloat16
MESH = pl.DeviceIdType.MESH


class Plan:
    def __init__(self, ring):
        self.ring = ring
        self.times = ring * TIMES
        self.blocks = ring // 2
        self.tall = TALL * ACROSS // self.blocks
        self.units = TIMES * (self.tall + 1) // PARTS
        self.tokens = self.times * SPAN
        self.group = self.times * 4
        self.frames = self.times // 2


def index(count):
    return lax.broadcasted_iota(jnp.int32, (count, 1), 0)


def among(value, low, high):
    return (value >= low) & (value < high)


def one_hot(target, width):
    lane = lax.broadcasted_iota(jnp.int32, (target.shape[0], width), 1)
    return jnp.where(lane == target, 1.0, 0.0).astype(BF16)


def strip_rows():
    row = index(128)
    side, rest = row >> 5, row & 31
    target = (rest >> 1) * ROWS + (1 - side) * (ROWS - 2) + (rest & 1)
    used = (rest < 2 * CHANS * FRAMES) & (side < 2)
    return one_hot(jnp.where(used, target, -1), CHANS * FRAMES * ROWS)


def unit_rows():
    row = index(UNITS * UNIT)
    unit, k = row >> 5, row & 31
    late = jnp.where(unit >= TALL + 1, 1, 0)
    plane = (k >> 3) * FRAMES + 2 * late + ((k >> 2) & 1)
    at = (unit - late * (TALL + 1)) * BLOCK + (k & 3) - 2
    used = (unit < 2 * (TALL + 1)) & (k < 24)
    main = jnp.where(used & among(at, 0, ROWS), plane * ROWS + at, -1)
    halo = jnp.where(at < 0, plane * 2 + at + 2, 32 + plane * 2 + at - ROWS)
    halo = jnp.where(used & ~among(at, 0, ROWS), halo, -1)
    return one_hot(main, CHANS * FRAMES * ROWS), one_hot(halo, 128)


def edge_columns():
    row = index(32)
    line = row & 15
    return one_hot(jnp.where(line < 2, line + (1 - (row >> 4)) * (COLS - 2), -1), COLS)


def block_columns():
    row = index(BLOCK * STEPS)
    c = sum(jnp.where(row >= n * STEPS, 1, 0) for n in range(1, BLOCK))
    x = row - c * STEPS
    at = x * BLOCK + c - 2
    main = jnp.where(among(at, 0, COLS), at, -1)
    halo = jnp.where(at < 0, at + 2, jnp.where(x <= WIDE, 16 + at - COLS, -1))
    return one_hot(main, COLS), one_hot(jnp.where(among(at, 0, COLS), -1, halo), 32)


def unit_lanes():
    row = index(512)
    k = row & 31
    target = ((row >> 5) & 3) * 128 + (row >> 7) * 24 + k
    return one_hot(jnp.where(k < 24, target, -1), 512)


def part_rows(plan):
    row = index(LINES)
    late = jnp.where(row >= AHEAD, 1, 0)
    below = row - late * AHEAD
    third = (below * 171) >> 9
    piece = below - 3 * third

    def source(item):
        unit = (item * 3856) >> 16
        return unit * 32 + item - unit * (SPAN + 1)

    width = plan.units * 32
    every = [one_hot(source(row + 5 * late), width)]
    used = (late == 1) | (below < 15)
    for n in range(3):
        item = jnp.where(late == 1, 69, 16) + third
        every.append(one_hot(jnp.where(used & (piece == n), source(item), -1), width))
    return jnp.concatenate(every, axis=0)


def spare_lanes():
    lane = index(128)
    every = [one_hot(jnp.where(lane < DENSE, lane, -1), 128)]
    for piece in range(3):
        at = lane - piece * SPARE
        every.append(one_hot(jnp.where(among(at, 0, SPARE), DENSE + at, -1), 128))
    return jnp.concatenate(every, axis=0)


def part_lanes():
    lane = index(128)
    every = [one_hot(jnp.where(lane < DENSE, lane, -1), 128)]
    for piece in range(3):
        every.append(one_hot(jnp.where(lane >= DENSE, lane - DENSE + piece * SPARE, -1), 128))
    return jnp.concatenate(every, axis=1)


def window_rows(first, units, lines):
    row = index(units * 32)
    item = (first + (row >> 5)) * (SPAN + 1) + (row & 15) + ((row >> 4) & 1)
    main = jnp.where(item < 16, item, jnp.where(among(item, 21, 69), item - 5, -1))
    total = one_hot(main, 4 * lines)
    rest = jnp.where(item < 69, 3 * (item - 16), AHEAD + 3 * (item - 69))
    for piece in range(3):
        at = (1 + piece) * lines + rest + piece
        total += one_hot(jnp.where(main < 0, at, -1), 4 * lines)
    return total


def tap_signs(out_pixel):
    i, j = divmod(out_pixel, 2)
    row = index(512)
    lane = row & 127
    c = sum(jnp.where(lane >= n * 24, 1, 0) for n in range(1, BLOCK))
    k = lane - c * 24
    up, along = ((row >> 8) & 1) * 4 + (k & 3), ((row >> 7) & 1) * 4 + c
    q, r = (up >> 1) - i, (along >> 1) - j
    used = among(q, 0, 3) & among(r, 0, 3) & (lane < DENSE)
    base = jnp.where(used, (q * 3 + r) * 24 + (k >> 3) * 8, 1024)
    odd = ((k >> 2) & 1) * 4 + (up & 1) * 2 + (along & 1)
    band = lax.broadcasted_iota(jnp.int32, (512, 216), 1) - base
    flips = band & odd
    sign = jnp.where(((flips ^ (flips >> 1) ^ (flips >> 2)) & 1) == 1, -1.0, 1.0)
    return jnp.where(among(band, 0, 8), sign, 0.0).astype(BF16)


def merge_order():
    row = index(WIDTH)
    return one_hot((row & 127) * 4 + (row >> 7), WIDTH)


def turned(plan):
    row = index(plan.tokens)
    part = row // plan.group
    rest = row - part * plan.group
    return one_hot((rest >> 2) * SPAN + part * 4 + (rest & 3), plan.tokens)


def turned_back(plan):
    row = index(plan.frames * SPAN)
    target = ((row >> 2) & 3) * (plan.frames * 4) + (row >> 4) * 4 + (row & 3)
    return one_hot(target, plan.frames * SPAN)


def frame_of(plan, start, step):
    return (start + plan.times + step) & (plan.times - 1)


def window_of(plan, start):
    row = index(plan.frames * SPAN)
    return one_hot(frame_of(plan, start, row >> 4) * SPAN + (row & 15), plan.tokens)


def window_turned(plan, start):
    row = index(plan.frames * SPAN)
    part = row // (plan.frames * 4)
    rest = row - part * plan.frames * 4
    frame = frame_of(plan, start, rest >> 2)
    return one_hot(frame * SPAN + part * 4 + (rest & 3), plan.tokens)


def dot(a, b):
    return jnp.dot(a, b, preferred_element_type=jnp.float32)


def dot_t(a, b):
    return lax.dot_general(a, b, (((1,), (1,)), ((), ())), preferred_element_type=jnp.float32)


def kernel(
    plan, counts,
    video_in, w_conv_in, w_merge_in, w_qkv_in, w_out_in,
    out,
    video, w_conv, w_merge, w_qkv, w_out,
    rows_out, rows_in, cols_out, cols_in, corners_out, corners_in,
    parts_out, parts_in,
    patches, taps, merge, latent, normed, queries, keys, values, mixed, encoded, turn, back, values_weight,
    loaded, rows_sent, rows_got, cols_sent, cols_got, corners_sent, corners_got,
    parts_sent, parts_got, out_sent, out_got, own_done,
):
    ring = plan.ring
    me, high, side = lax.axis_index("tm"), lax.axis_index("height"), lax.axis_index("width")
    highs, sides = counts
    above, below = lax.rem(high + highs - 1, highs), lax.rem(high + 1, highs)
    before, after = lax.rem(side + sides - 1, sides), lax.rem(side + 1, sides)

    loads = [
        pltpu.make_async_copy(source, target, loaded.at[n])
        for n, (source, target) in enumerate(
            (
                (video_in, video), (w_conv_in, w_conv), (w_merge_in, w_merge),
                (w_qkv_in, w_qkv), (w_out_in, w_out),
            )
        )
    ]
    loads[0].start()

    barrier = pltpu.get_barrier_semaphore()
    beside = [{"height": peer} for peer in (above, below)]
    beside += [{"width": peer} for peer in (before, after)]
    beside += [{"height": u, "width": v} for u in (above, below) for v in (before, after)]
    for peer in beside:
        pl.semaphore_signal(barrier, inc=1, device_id=peer, device_id_type=MESH)

    def greet(k, _):
        peer = lax.rem(me + k, ring)
        pl.semaphore_signal(barrier, inc=1, device_id={"tm": peer}, device_id_type=MESH)
        return 0

    lax.fori_loop(1, ring, greet, 0)
    for load in loads[1:]:
        load.start()

    strip, edge = strip_rows(), edge_columns()
    unit_main, unit_halo = unit_rows()
    block_main, block_halo = block_columns()
    loads[0].wait()
    pixels = video[...].reshape(CHANS * FRAMES * ROWS, COLS)
    strips = dot(strip, pixels).astype(BF16)
    rows_out[0] = strips[:32]
    rows_out[1] = strips[32:64]
    edges = dot_t(edge, pixels).astype(BF16)
    cols_out[0] = edges[:16]
    cols_out[1] = edges[16:]
    corners = dot_t(edge, strips).astype(BF16)
    corners_out[0] = corners[:16]
    corners_out[1] = corners[16:]
    pl.semaphore_wait(barrier, ring - 1 + len(beside))

    def border_copy(source, target, sent, got, at, into, peer):
        return pltpu.make_async_remote_copy(
            src_ref=source.at[at], dst_ref=target.at[into], send_sem=sent.at[into],
            recv_sem=got.at[into], device_id=peer, device_id_type=MESH,
        )

    border_copies = []
    for down, u in enumerate((below, above)):
        border_copies.append(
            border_copy(rows_out, rows_in, rows_sent, rows_got, down, down, {"height": u})
        )
    for along, v in enumerate((after, before)):
        border_copies.append(
            border_copy(cols_out, cols_in, cols_sent, cols_got, along, along, {"width": v})
        )
    for down, u in enumerate((below, above)):
        for along, v in enumerate((after, before)):
            border_copies.append(
                border_copy(
                    corners_out, corners_in, corners_sent, corners_got, along, down * 2 + along,
                    {"height": u, "width": v},
                )
            )
    for copy in border_copies:
        copy.start()
    inner = dot(unit_main, pixels)
    lanes = unit_lanes()
    place, spare = part_rows(plan), spare_lanes()
    for copy in border_copies:
        copy.wait()

    def kept(value, condition):
        return jnp.where(condition, value, jnp.zeros_like(value))

    has_rows, has_cols = (high > 0, high < highs - 1), (side > 0, side < sides - 1)
    halo = [kept(rows_in[n], has_rows[n]) for n in range(2)]
    halo = jnp.concatenate(halo + [jnp.zeros((64, COLS), BF16)], axis=0)
    units = (inner + dot(unit_halo, halo)).astype(BF16)
    cols = jnp.concatenate([kept(cols_in[n], has_cols[n]) for n in range(2)], axis=0)
    strip_lane = lax.broadcasted_iota(jnp.int32, (16, 128), 1)
    corner = jnp.concatenate(
        [
            jnp.where(
                strip_lane < 32,
                kept(corners_in[n], has_rows[0] & has_cols[n]),
                kept(corners_in[2 + n], has_rows[1] & has_cols[n]),
            )
            for n in range(2)
        ],
        axis=0,
    )
    sidelong = (dot_t(cols, unit_main) + dot_t(corner, unit_halo)).astype(BF16)
    spread = (dot_t(block_main, units) + dot(block_halo, sidelong)).astype(BF16)

    stacked = jnp.concatenate(
        [
            jnp.concatenate(
                [spread[c * STEPS : (c + 1) * STEPS, q * 128 : (q + 1) * 128] for c in range(4)], axis=1
            )
            for q in range(UNITS // 4)
        ],
        axis=0,
    )
    stacked = dot(stacked, lanes).astype(BF16)

    def piece(t, up, jx):
        q, u = divmod(t * (TALL + 1) + up, 4)
        start = q * STEPS + jx * SPAN
        return stacked[start : start + 32, u * 128 : (u + 1) * 128]

    def pack(part):
        every = []
        for block in range(plan.blocks):
            jy, jx = divmod(block, ACROSS)
            pieces = []
            for unit in range(part * plan.units, (part + 1) * plan.units):
                up, t = divmod(unit, TIMES)
                pieces.append(piece(t, jy * plan.tall + up, jx))
            every.append(jnp.concatenate(pieces, axis=0))
        placed = dot(place, jnp.concatenate(every, axis=1)).astype(BF16)
        placed = [
            jnp.concatenate(
                [
                    placed[n * LINES : (n + 1) * LINES, block * 128 : (block + 1) * 128]
                    for n in range(4)
                ],
                axis=1,
            )
            for block in range(plan.blocks)
        ]
        return dot(jnp.concatenate(placed, axis=0), spare).astype(BF16)

    stages = ((0, 0, LINES), (1, 0, AHEAD), (1, AHEAD, LINES - AHEAD))

    def part_copy(stage, source, target):
        part, start, count = stages[stage]
        return pltpu.make_async_remote_copy(
            src_ref=parts_out.at[part, lax.rem(target, plan.blocks), pl.ds(start, count)],
            dst_ref=parts_in.at[part, source, pl.ds(start, count)],
            send_sem=parts_sent.at[stage, target], recv_sem=parts_got.at[stage, source],
            device_id={"tm": target}, device_id_type=MESH,
        )

    def ahead_by(k):
        step = ring - k
        ahead = (step + 1) // 2
        return lax.select(lax.rem(step, 2) == 1, ahead, ring - ahead)

    def send_parts(stage):
        def send(k, _):
            part_copy(stage, me, lax.rem(me + ahead_by(k), ring)).start()
            return 0

        lax.fori_loop(1, ring, send, 0)

    for part in range(PARTS):
        packed = pack(part)
        for block in range(plan.blocks):
            parts_out[part, block] = packed[block * LINES : (block + 1) * LINES]
        for stage in ((0,), (1, 2))[part]:
            send_parts(stage)
        parts_in[part, me] = parts_out[part, lax.rem(me, plan.blocks)]

    loads[1].wait()
    for out_pixel in range(4):
        signs = tap_signs(out_pixel)
        for dt in range(3):
            taps[dt * WIDTH : (dt + 1) * WIDTH, out_pixel * 128 : (out_pixel + 1) * 128] = (
                dot(signs, w_conv[dt]) * (1.0 / math.sqrt(8.0))
            ).astype(BF16)
    loads[2].wait()
    merge[...] = dot(merge_order(), w_merge[...]).astype(BF16)
    turn[: plan.tokens] = turned(plan)
    back[...] = turned_back(plan)
    for y in range(plan.tall):
        patches[y, 0 : 2 * SPAN, :] = jnp.zeros((2 * SPAN, WIDTH), BF16)
    loads[3].wait()
    values_weight[...] = dot_t(one_hot(index(WIDTH), WIDTH), w_qkv[:, 2 * WIDTH :]).astype(BF16)
    loads[4].wait()

    apart = part_lanes()

    def take(stage):
        part, start, count = stages[stage]
        lines = start + count
        first, units = ((0, plan.units), (0, 1), (1, plan.units - 1))[stage]
        batch = (4, 16, 8)[stage]
        pick = window_rows(first, units, lines)

        def one(k, _):
            sources = []
            for n in range(batch):
                at = k * batch + n + 1
                source = lax.rem(me + ahead_by(at), ring)
                sources.append(source)

                @pl.when(at < ring)
                def _():
                    part_copy(stage, source, me).wait_recv()

            rows = jnp.concatenate([parts_in[part, source, :lines] for source in sources], axis=0)
            rows = dot(rows, apart).astype(BF16)
            rows = jnp.concatenate(
                [
                    jnp.concatenate(
                        [
                            rows[n * lines : (n + 1) * lines, copy * 128 : (copy + 1) * 128]
                            for copy in range(4)
                        ],
                        axis=0,
                    )
                    for n in range(batch)
                ],
                axis=1,
            )
            windows = dot(pick, rows).astype(BF16)
            for n, source in enumerate(sources):
                for unit in range(units):
                    up, t = divmod(part * plan.units + first + unit, TIMES)
                    at = pl.multiple_of((source * TIMES + t + 2) * SPAN, SPAN)
                    for dx in range(2):
                        row = unit * 32 + dx * SPAN
                        value = windows[row : row + SPAN, n * 128 : (n + 1) * 128]
                        for dy in range(2):
                            if 0 <= up - dy < plan.tall:
                                tap = dy * 2 + dx
                                patches[
                                    up - dy, pl.ds(at, SPAN), tap * 128 : (tap + 1) * 128
                                ] = value
            return 0

        lax.fori_loop(0, ring // batch, one, 0)

    half = plan.tokens // 2
    group = plan.group
    lane = lax.broadcasted_iota(jnp.int32, (1, 128), 1)
    head_scale = [
        jnp.where((lane < 64) == (head == 0), 0.125, 0.0).astype(BF16) for head in range(2)
    ]
    some = plan.frames * 4
    query_at = lax.broadcasted_iota(jnp.int32, (group, 2 * some), 1) & (some - 1)
    key_at = lax.broadcasted_iota(jnp.int32, (group, 2 * some), 0)
    same = (query_at & 3) == (key_at & 3)

    far = ring // 4
    start = (me - far) * TIMES + 1
    turn[plan.tokens :] = window_turned(plan, start)
    window = window_of(plan, start)
    allowed = same & (frame_of(plan, start, query_at >> 2) >= (key_at >> 2))

    def place_of(source, y, first, count):
        block = lax.rem(source, plan.blocks)
        line = (block // ACROSS) * plan.tall + y
        column = pl.multiple_of(lax.rem(block, ACROSS) * SPAN, SPAN)
        return out.at[pl.ds(first, count), line, pl.ds(column, SPAN), :]

    def out_copies(y, source_of):
        copies = []
        for slot, ahead in enumerate(reach):
            source = source_of(ahead)
            first, count = (0, 1) if ahead == far else (1, 1) if ahead == -far else (0, TIMES)
            at = max(0, (ahead + far) * TIMES - 1)
            copies.append(
                pltpu.make_async_remote_copy(
                    src_ref=encoded.at[y, pl.ds(at, count)],
                    dst_ref=place_of(source, y, first, count),
                    send_sem=out_sent.at[y, slot], recv_sem=out_got.at[y, slot],
                    device_id={"tm": lax.rem(source + ahead + ring, ring)}, device_id_type=MESH,
                )
            )
        return copies

    reach = [way * ahead for ahead in range(far, 0, -1) for way in (1, -1)]

    def own_copy(y):
        return pltpu.make_async_copy(
            encoded.at[y, pl.ds(far * TIMES - 1, TIMES)], place_of(me, y, 0, TIMES), own_done.at[y]
        )

    def one_row(y, _):
        for stage in range(len(stages)):
            pl.when(y == stage)(functools.partial(take, stage))

        for m in range(2):
            at = m * half
            around = [patches[y, at + dt * SPAN : at + dt * SPAN + half, :] for dt in range(3)]
            total = 0.5 * dot(jnp.concatenate(around, axis=1), taps[...])
            active = (total + total * jnp.tanh(total)).astype(BF16)
            value = dot(active, merge[...]).astype(BF16)
            latent[at : at + half, :] = value
            wide = value.astype(jnp.float32)
            meansq = jnp.mean(wide * wide, axis=-1, keepdims=True)
            normed[at : at + half, :] = (wide * lax.rsqrt(meansq + 1e-06)).astype(BF16)

        tokens = dot(turn[...], normed[...]).astype(BF16)
        queries[...] = dot(tokens[plan.tokens :], w_qkv[:, :WIDTH]).astype(BF16)
        tokens = tokens[: plan.tokens]
        keys[...] = dot(tokens, w_qkv[:, WIDTH : 2 * WIDTH]).astype(BF16)
        values[...] = dot_t(values_weight[...], tokens).astype(BF16)

        def attended(part, pair):
            columns = slice(pair * 128, (pair + 1) * 128)
            rows = slice(part * group, (part + 1) * group)
            query = queries[part * some : (part + 1) * some, columns]
            both = jnp.concatenate([query * head_scale[0], query * head_scale[1]], axis=0)
            scores = jnp.where(allowed, dot_t(keys[rows, columns], both), -1e30)
            expon = jnp.exp(scores - jnp.max(scores, axis=0, keepdims=True))
            share = 1.0 / jnp.sum(expon, axis=0, keepdims=True)
            return dot(values[columns, rows], expon.astype(BF16)) * share

        for part in range(0, SPAN // 4, 2):
            for pair in range(HEADS // 2):
                left, right = attended(part, pair), attended(part + 1, pair)
                upper = jnp.where(lane < 64, left[:64], pltpu.roll(right[:64], 64, axis=1))
                lower = jnp.where(lane < 64, pltpu.roll(left[64:], 64, axis=1), right[64:])
                mixed[pair * 128 : (pair + 1) * 128, part * some : (part + 2) * some] = (
                    jnp.concatenate([upper, lower], axis=0).astype(BF16)
                )

        straight = dot_t(back[...], mixed[...]).astype(BF16)
        total = dot(straight, w_out[...]) + dot(window, latent[...])
        encoded[y] = total.astype(BF16).reshape(plan.frames, SPAN, WIDTH)

        for copy in out_copies(y, lambda ahead: me):
            copy.start()
        own_copy(y).start()
        return 0

    lax.fori_loop(0, plan.tall, one_row, 0)

    def parts_left(k, _):
        for stage in range(len(stages)):
            part_copy(stage, me, lax.rem(me + ahead_by(k), ring)).wait_send()
        return 0

    lax.fori_loop(1, ring, parts_left, 0)

    def all_done(y, _):
        for copy in out_copies(y, lambda ahead: me):
            copy.wait_send()
        for copy in out_copies(y, lambda ahead: lax.rem(me - ahead + ring, ring)):
            copy.wait_recv()
        own_copy(y).wait()
        return 0

    lax.fori_loop(0, plan.tall, all_done, 0)


def copied(value):
    def body(source, target, done):
        rows = value.shape[1]
        copies = []
        for n in range(COPIES):
            at = (n // (COPIES // 2), pl.ds(n % (COPIES // 2) * (rows // (COPIES // 2)), rows // (COPIES // 2)))
            copies.append(pltpu.make_async_copy(source.at[at], target.at[at], done.at[n]))
        for copy in copies:
            copy.start()
        for copy in copies:
            copy.wait()

    return pl.pallas_call(
        body,
        out_shape=jax.ShapeDtypeStruct(value.shape, value.dtype),
        in_specs=[pl.BlockSpec(memory_space=pltpu.VMEM)],
        out_specs=pl.BlockSpec(memory_space=pl.ANY),
        scratch_shapes=[pltpu.SemaphoreType.DMA((COPIES,))],
        compiler_params=pltpu.CompilerParams(vmem_limit_bytes=2**20),
    )(value)


def solution(mesh):
    plan = Plan(mesh.shape["tm"])
    counts = (mesh.shape["height"], mesh.shape["width"])

    def shards(video, w_conv, w_merge, w_qkv, w_out):
        operands = (video, w_conv.reshape(3, 216, 128), w_merge, w_qkv, w_out)
        dma = pltpu.SemaphoreType.DMA
        held = [pltpu.VMEM(one.shape, BF16) for one in operands]
        buffers = [
            (2, 32, COLS), (2, 32, COLS),
            (2, 16, CHANS * FRAMES * ROWS), (2, 16, CHANS * FRAMES * ROWS),
            (2, 16, 128), (4, 16, 128),
            (PARTS, plan.blocks, LINES, 128), (PARTS, plan.ring, LINES, 128),
            (plan.tall, plan.tokens + 2 * SPAN, WIDTH),
            (3 * WIDTH, WIDTH), (WIDTH, WIDTH),
            (plan.tokens, WIDTH), (plan.tokens, WIDTH),
            (plan.frames * SPAN, WIDTH), (plan.tokens, WIDTH), (WIDTH, plan.tokens),
            (WIDTH, plan.frames * SPAN),
            (plan.tall, plan.frames, SPAN, WIDTH),
            (plan.tokens + plan.frames * SPAN, plan.tokens), (plan.frames * SPAN, plan.frames * SPAN),
            (WIDTH, WIDTH),
        ]
        semaphores = [
            (len(operands),), (2,), (2,), (2,), (2,), (4,), (4,),
            (PARTS + 1, plan.ring), (PARTS + 1, plan.ring),
            (plan.tall, plan.ring // 2), (plan.tall, plan.ring // 2), (plan.tall,),
        ]
        return copied(pl.pallas_call(
            functools.partial(kernel, plan, counts),
            out_shape=pltpu.VMEM((TIMES, TALL, WIDE, WIDTH), BF16),
            in_specs=[pl.BlockSpec(memory_space=pltpu.HBM)] * len(operands),
            out_specs=pl.BlockSpec(memory_space=pl.ANY),
            scratch_shapes=held
            + [pltpu.VMEM(shape, BF16) for shape in buffers]
            + [dma(shape) for shape in semaphores],
            compiler_params=pltpu.CompilerParams(
                collective_id=0, has_side_effects=True, vmem_limit_bytes=56 * 2**20
            ),
            cost_estimate=pl.CostEstimate(
                flops=8 * 10**9, bytes_accessed=6 * 10**6, transcendentals=2 * 10**6
            ),
        )(*operands))

    return jax.shard_map(
        shards,
        mesh=mesh,
        in_specs=(P(None, "tm", "height", "width"), P(), P(), P(), P()),
        out_specs=P("tm", "height", "width", None),
        check_vma=False,
    )
```

```python
import functools
import math

import jax
import jax.numpy as jnp
from jax import lax
from jax.experimental import pallas as pl
from jax.experimental.pallas import tpu as pltpu
from jax.sharding import PartitionSpec as P

HEADS = 8

CHANS, FRAMES, ROWS, COLS = 3, 4, 32, 256
TIMES = FRAMES // 2
BLOCK = 4
TALL, WIDE = ROWS // BLOCK, COLS // BLOCK
SPAN = 16
ACROSS = WIDE // SPAN
UNIT = 32
STEPS = 80
UNITS = 20
WIDTH = 512
PARTS = 2
LINES = 64
AHEAD = 16
COPIES = 8
EARLY = (5, 6)
DENSE = 96
SPARE = 32
BF16 = jnp.bfloat16
MESH = pl.DeviceIdType.MESH


class Plan:
    def __init__(self, ring):
        self.ring = ring
        self.times = ring * TIMES
        self.blocks = ring // 2
        self.tall = TALL * ACROSS // self.blocks
        self.units = TIMES * (self.tall + 1) // PARTS
        self.tokens = self.times * SPAN
        self.group = self.times * 4
        self.frames = self.times // 2


def index(count):
    return lax.broadcasted_iota(jnp.int32, (count, 1), 0)


def among(value, low, high):
    return (value >= low) & (value < high)


def one_hot(target, width):
    lane = lax.broadcasted_iota(jnp.int32, (target.shape[0], width), 1)
    return jnp.where(lane == target, 1.0, 0.0).astype(BF16)


def strip_rows():
    row = index(128)
    side, rest = row >> 5, row & 31
    target = (rest >> 1) * ROWS + (1 - side) * (ROWS - 2) + (rest & 1)
    used = (rest < 2 * CHANS * FRAMES) & (side < 2)
    return one_hot(jnp.where(used, target, -1), CHANS * FRAMES * ROWS)


def unit_rows():
    row = index(UNITS * UNIT)
    unit, k = row >> 5, row & 31
    late = jnp.where(unit >= TALL + 1, 1, 0)
    plane = (k >> 3) * FRAMES + 2 * late + ((k >> 2) & 1)
    at = (unit - late * (TALL + 1)) * BLOCK + (k & 3) - 2
    used = (unit < 2 * (TALL + 1)) & (k < 24)
    main = jnp.where(used & among(at, 0, ROWS), plane * ROWS + at, -1)
    halo = jnp.where(at < 0, plane * 2 + at + 2, 32 + plane * 2 + at - ROWS)
    halo = jnp.where(used & ~among(at, 0, ROWS), halo, -1)
    return one_hot(main, CHANS * FRAMES * ROWS), one_hot(halo, 128)


def edge_columns():
    row = index(32)
    line = row & 15
    return one_hot(jnp.where(line < 2, line + (1 - (row >> 4)) * (COLS - 2), -1), COLS)


def block_columns():
    row = index(BLOCK * STEPS)
    c = sum(jnp.where(row >= n * STEPS, 1, 0) for n in range(1, BLOCK))
    x = row - c * STEPS
    at = x * BLOCK + c - 2
    main = jnp.where(among(at, 0, COLS), at, -1)
    halo = jnp.where(at < 0, at + 2, jnp.where(x <= WIDE, 16 + at - COLS, -1))
    return one_hot(main, COLS), one_hot(jnp.where(among(at, 0, COLS), -1, halo), 32)


def unit_lanes():
    row = index(512)
    k = row & 31
    target = ((row >> 5) & 3) * 128 + (row >> 7) * 24 + k
    return one_hot(jnp.where(k < 24, target, -1), 512)


def part_rows(plan):
    row = index(LINES)
    late = jnp.where(row >= AHEAD, 1, 0)
    below = row - late * AHEAD
    third = (below * 171) >> 9
    piece = below - 3 * third

    def source(item):
        unit = (item * 3856) >> 16
        return unit * 32 + item - unit * (SPAN + 1)

    width = plan.units * 32
    every = [one_hot(source(row + 5 * late), width)]
    used = (late == 1) | (below < 15)
    for n in range(3):
        item = jnp.where(late == 1, 69, 16) + third
        every.append(one_hot(jnp.where(used & (piece == n), source(item), -1), width))
    return jnp.concatenate(every, axis=0)


def spare_lanes():
    lane = index(128)
    every = [one_hot(jnp.where(lane < DENSE, lane, -1), 128)]
    for piece in range(3):
        at = lane - piece * SPARE
        every.append(one_hot(jnp.where(among(at, 0, SPARE), DENSE + at, -1), 128))
    return jnp.concatenate(every, axis=0)


def part_lanes():
    lane = index(128)
    every = [one_hot(jnp.where(lane < DENSE, lane, -1), 128)]
    for piece in range(3):
        every.append(one_hot(jnp.where(lane >= DENSE, lane - DENSE + piece * SPARE, -1), 128))
    return jnp.concatenate(every, axis=1)


def window_rows(first, units, lines):
    row = index(units * 32)
    item = (first + (row >> 5)) * (SPAN + 1) + (row & 15) + ((row >> 4) & 1)
    main = jnp.where(item < 16, item, jnp.where(among(item, 21, 69), item - 5, -1))
    total = one_hot(main, 4 * lines)
    rest = jnp.where(item < 69, 3 * (item - 16), AHEAD + 3 * (item - 69))
    for piece in range(3):
        at = (1 + piece) * lines + rest + piece
        total += one_hot(jnp.where(main < 0, at, -1), 4 * lines)
    return total


def tap_signs(out_pixel):
    i, j = divmod(out_pixel, 2)
    row = index(512)
    lane = row & 127
    c = sum(jnp.where(lane >= n * 24, 1, 0) for n in range(1, BLOCK))
    k = lane - c * 24
    up, along = ((row >> 8) & 1) * 4 + (k & 3), ((row >> 7) & 1) * 4 + c
    q, r = (up >> 1) - i, (along >> 1) - j
    used = among(q, 0, 3) & among(r, 0, 3) & (lane < DENSE)
    base = jnp.where(used, (q * 3 + r) * 24 + (k >> 3) * 8, 1024)
    odd = ((k >> 2) & 1) * 4 + (up & 1) * 2 + (along & 1)
    band = lax.broadcasted_iota(jnp.int32, (512, 216), 1) - base
    flips = band & odd
    sign = jnp.where(((flips ^ (flips >> 1) ^ (flips >> 2)) & 1) == 1, -1.0, 1.0)
    return jnp.where(among(band, 0, 8), sign, 0.0).astype(BF16)


def merge_order():
    row = index(WIDTH)
    return one_hot((row & 127) * 4 + (row >> 7), WIDTH)


def turned(plan):
    row = index(plan.tokens)
    part = row // plan.group
    rest = row - part * plan.group
    return one_hot((rest >> 2) * SPAN + part * 4 + (rest & 3), plan.tokens)


def turned_back(plan):
    row = index(plan.frames * SPAN)
    target = ((row >> 2) & 3) * (plan.frames * 4) + (row >> 4) * 4 + (row & 3)
    return one_hot(target, plan.frames * SPAN)


def frame_of(plan, start, step):
    return (start + plan.times + step) & (plan.times - 1)


def window_of(plan, start):
    row = index(plan.frames * SPAN)
    return one_hot(frame_of(plan, start, row >> 4) * SPAN + (row & 15), plan.tokens)


def window_turned(plan, start):
    row = index(plan.frames * SPAN)
    part = row // (plan.frames * 4)
    rest = row - part * plan.frames * 4
    frame = frame_of(plan, start, rest >> 2)
    return one_hot(frame * SPAN + part * 4 + (rest & 3), plan.tokens)


def dot(a, b):
    return jnp.dot(a, b, preferred_element_type=jnp.float32)


def dot_t(a, b):
    return lax.dot_general(a, b, (((1,), (1,)), ((), ())), preferred_element_type=jnp.float32)


def kernel(
    plan, counts,
    video_in, w_conv_in, w_merge_in, w_qkv_in, w_out_in,
    out,
    video, w_conv, w_merge, w_qkv, w_out,
    rows_out, rows_in, cols_out, cols_in, corners_out, corners_in,
    parts_out, parts_in,
    patches, taps, merge, latent, normed, queries, keys, values, mixed, encoded, turn, back, values_weight,
    loaded, rows_sent, rows_got, cols_sent, cols_got, corners_sent, corners_got,
    parts_sent, parts_got, out_sent, out_got, own_done,
):
    ring = plan.ring
    me, high, side = lax.axis_index("tm"), lax.axis_index("height"), lax.axis_index("width")
    highs, sides = counts
    above, below = lax.rem(high + highs - 1, highs), lax.rem(high + 1, highs)
    before, after = lax.rem(side + sides - 1, sides), lax.rem(side + 1, sides)

    loads = [
        pltpu.make_async_copy(source, target, loaded.at[n])
        for n, (source, target) in enumerate(
            (
                (video_in, video), (w_conv_in, w_conv), (w_merge_in, w_merge),
                (w_qkv_in, w_qkv), (w_out_in, w_out),
            )
        )
    ]
    loads[0].start()

    barrier = pltpu.get_barrier_semaphore()
    beside = [{"height": peer} for peer in (above, below)]
    beside += [{"width": peer} for peer in (before, after)]
    beside += [{"height": u, "width": v} for u in (above, below) for v in (before, after)]
    for peer in beside:
        pl.semaphore_signal(barrier, inc=1, device_id=peer, device_id_type=MESH)

    def greet(k, _):
        peer = lax.rem(me + k, ring)
        pl.semaphore_signal(barrier, inc=1, device_id={"tm": peer}, device_id_type=MESH)
        return 0

    lax.fori_loop(1, ring, greet, 0)
    for load in loads[1:]:
        load.start()

    strip, edge = strip_rows(), edge_columns()
    unit_main, unit_halo = unit_rows()
    block_main, block_halo = block_columns()
    loads[0].wait()
    pixels = video[...].reshape(CHANS * FRAMES * ROWS, COLS)
    strips = dot(strip, pixels).astype(BF16)
    rows_out[0] = strips[:32]
    rows_out[1] = strips[32:64]
    edges = dot_t(edge, pixels).astype(BF16)
    cols_out[0] = edges[:16]
    cols_out[1] = edges[16:]
    corners = dot_t(edge, strips).astype(BF16)
    corners_out[0] = corners[:16]
    corners_out[1] = corners[16:]
    pl.semaphore_wait(barrier, ring - 1 + len(beside))

    def border_copy(source, target, sent, got, at, into, peer):
        return pltpu.make_async_remote_copy(
            src_ref=source.at[at], dst_ref=target.at[into], send_sem=sent.at[into],
            recv_sem=got.at[into], device_id=peer, device_id_type=MESH,
        )

    border_copies = []
    for down, u in enumerate((below, above)):
        border_copies.append(
            border_copy(rows_out, rows_in, rows_sent, rows_got, down, down, {"height": u})
        )
    for along, v in enumerate((after, before)):
        border_copies.append(
            border_copy(cols_out, cols_in, cols_sent, cols_got, along, along, {"width": v})
        )
    for down, u in enumerate((below, above)):
        for along, v in enumerate((after, before)):
            border_copies.append(
                border_copy(
                    corners_out, corners_in, corners_sent, corners_got, along, down * 2 + along,
                    {"height": u, "width": v},
                )
            )
    for copy in border_copies:
        copy.start()
    inner = dot(unit_main, pixels)
    lanes = unit_lanes()
    place, spare = part_rows(plan), spare_lanes()

    def stack(spread):
        quads = [
            jnp.concatenate(
                [spread[c * STEPS : (c + 1) * STEPS, q * 128 : (q + 1) * 128] for c in range(4)], axis=1
            )
            for q in range(spread.shape[1] // 128)
        ]
        return dot(jnp.concatenate(quads, axis=0), lanes).astype(BF16)

    def pack(stacked, quads, part, blocks):
        every = []
        for block in blocks:
            jy, jx = divmod(block, ACROSS)
            pieces = []
            for unit in range(part * plan.units, (part + 1) * plan.units):
                up, t = divmod(unit, TIMES)
                q, u = divmod(t * (TALL + 1) + jy * plan.tall + up, 4)
                at = quads.index(q) * STEPS + jx * SPAN
                pieces.append(stacked[at : at + 32, u * 128 : (u + 1) * 128])
            every.append(jnp.concatenate(pieces, axis=0))
        placed = dot(place, jnp.concatenate(every, axis=1)).astype(BF16)
        placed = [
            jnp.concatenate(
                [placed[m * LINES : (m + 1) * LINES, n * 128 : (n + 1) * 128] for m in range(4)], axis=1
            )
            for n in range(len(blocks))
        ]
        packed = dot(jnp.concatenate(placed, axis=0), spare).astype(BF16)
        for n, block in enumerate(blocks):
            parts_out[part, block] = packed[n * LINES : (n + 1) * LINES]

    stages = ((0, 0, LINES), (1, 0, AHEAD), (1, AHEAD, LINES - AHEAD))

    def part_copy(stage, source, target):
        part, start, count = stages[stage]
        return pltpu.make_async_remote_copy(
            src_ref=parts_out.at[part, lax.rem(target, plan.blocks), pl.ds(start, count)],
            dst_ref=parts_in.at[part, source, pl.ds(start, count)],
            send_sem=parts_sent.at[stage, target], recv_sem=parts_got.at[stage, source],
            device_id={"tm": target}, device_id_type=MESH,
        )

    def ahead_by(k):
        step = ring - k
        ahead = (step + 1) // 2
        return lax.select(lax.rem(step, 2) == 1, ahead, ring - ahead)

    def send_parts(stage):
        def send(k, _):
            target = lax.rem(me + ahead_by(k), ring)

            @pl.when((stage > 0) | ~among(lax.rem(target, plan.blocks), EARLY[0], EARLY[-1] + 1))
            def _():
                part_copy(stage, me, target).start()

            return 0

        lax.fori_loop(1, ring, send, 0)

    quads = (1, 3)
    early = jnp.concatenate([inner[q * 128 : (q + 1) * 128] for q in quads], axis=0).astype(BF16)
    pack(stack(dot_t(block_main, early).astype(BF16)), quads, 0, EARLY)
    for target in range(ring):
        if target % plan.blocks in EARLY:

            @pl.when(me != target)
            def _():
                part_copy(0, me, target).start()

    for copy in border_copies:
        copy.wait()

    def kept(value, condition):
        return jnp.where(condition, value, jnp.zeros_like(value))

    has_rows, has_cols = (high > 0, high < highs - 1), (side > 0, side < sides - 1)
    halo = [kept(rows_in[n], has_rows[n]) for n in range(2)]
    halo = jnp.concatenate(halo + [jnp.zeros((64, COLS), BF16)], axis=0)
    units = (inner + dot(unit_halo, halo)).astype(BF16)
    cols = jnp.concatenate([kept(cols_in[n], has_cols[n]) for n in range(2)], axis=0)
    strip_lane = lax.broadcasted_iota(jnp.int32, (16, 128), 1)
    corner = jnp.concatenate(
        [
            jnp.where(
                strip_lane < 32,
                kept(corners_in[n], has_rows[0] & has_cols[n]),
                kept(corners_in[2 + n], has_rows[1] & has_cols[n]),
            )
            for n in range(2)
        ],
        axis=0,
    )
    sidelong = (dot_t(cols, unit_main) + dot_t(corner, unit_halo)).astype(BF16)
    spread = (dot_t(block_main, units) + dot(block_halo, sidelong)).astype(BF16)

    stacked, quads = stack(spread), tuple(range(UNITS // 4))
    pack(stacked, quads, 0, [block for block in range(plan.blocks) if block not in EARLY])
    send_parts(0)
    parts_in[0, me] = parts_out[0, lax.rem(me, plan.blocks)]
    pack(stacked, quads, 1, range(plan.blocks))
    send_parts(1)
    send_parts(2)
    parts_in[1, me] = parts_out[1, lax.rem(me, plan.blocks)]

    loads[1].wait()
    for out_pixel in range(4):
        signs = tap_signs(out_pixel)
        for dt in range(3):
            taps[dt * WIDTH : (dt + 1) * WIDTH, out_pixel * 128 : (out_pixel + 1) * 128] = (
                dot(signs, w_conv[dt]) * (1.0 / math.sqrt(8.0))
            ).astype(BF16)
    loads[2].wait()
    merge[...] = dot(merge_order(), w_merge[...]).astype(BF16)
    turn[: plan.tokens] = turned(plan)
    back[...] = turned_back(plan)
    for y in range(plan.tall):
        patches[y, 0 : 2 * SPAN, :] = jnp.zeros((2 * SPAN, WIDTH), BF16)
    loads[3].wait()
    values_weight[...] = dot_t(one_hot(index(WIDTH), WIDTH), w_qkv[:, 2 * WIDTH :]).astype(BF16)
    loads[4].wait()

    apart = part_lanes()

    def take(stage):
        part, start, count = stages[stage]
        lines = start + count
        first, units = ((0, plan.units), (0, 1), (1, plan.units - 1))[stage]
        batch = (4, 16, 8)[stage]
        pick = window_rows(first, units, lines)

        def one(k, _):
            sources = []
            for n in range(batch):
                at = k * batch + n + 1
                source = lax.rem(me + ahead_by(at), ring)
                sources.append(source)

                @pl.when(at < ring)
                def _():
                    part_copy(stage, source, me).wait_recv()

            rows = jnp.concatenate([parts_in[part, source, :lines] for source in sources], axis=0)
            rows = dot(rows, apart).astype(BF16)
            rows = jnp.concatenate(
                [
                    jnp.concatenate(
                        [
                            rows[n * lines : (n + 1) * lines, copy * 128 : (copy + 1) * 128]
                            for copy in range(4)
                        ],
                        axis=0,
                    )
                    for n in range(batch)
                ],
                axis=1,
            )
            windows = dot(pick, rows).astype(BF16)
            for n, source in enumerate(sources):
                for unit in range(units):
                    up, t = divmod(part * plan.units + first + unit, TIMES)
                    at = pl.multiple_of((source * TIMES + t + 2) * SPAN, SPAN)
                    for dx in range(2):
                        row = unit * 32 + dx * SPAN
                        value = windows[row : row + SPAN, n * 128 : (n + 1) * 128]
                        for dy in range(2):
                            if 0 <= up - dy < plan.tall:
                                tap = dy * 2 + dx
                                patches[
                                    up - dy, pl.ds(at, SPAN), tap * 128 : (tap + 1) * 128
                                ] = value
            return 0

        lax.fori_loop(0, ring // batch, one, 0)

    half = plan.tokens // 2
    group = plan.group
    lane = lax.broadcasted_iota(jnp.int32, (1, 128), 1)
    head_scale = [
        jnp.where((lane < 64) == (head == 0), 0.125, 0.0).astype(BF16) for head in range(2)
    ]
    some = plan.frames * 4
    query_at = lax.broadcasted_iota(jnp.int32, (group, 2 * some), 1) & (some - 1)
    key_at = lax.broadcasted_iota(jnp.int32, (group, 2 * some), 0)
    same = (query_at & 3) == (key_at & 3)

    far = ring // 4
    start = (me - far) * TIMES + 1
    turn[plan.tokens :] = window_turned(plan, start)
    window = window_of(plan, start)
    allowed = same & (frame_of(plan, start, query_at >> 2) >= (key_at >> 2))

    def place_of(source, y, first, count):
        block = lax.rem(source, plan.blocks)
        line = (block // ACROSS) * plan.tall + y
        column = pl.multiple_of(lax.rem(block, ACROSS) * SPAN, SPAN)
        return out.at[pl.ds(first, count), line, pl.ds(column, SPAN), :]

    def out_copies(y, source_of):
        copies = []
        for slot, ahead in enumerate(reach):
            source = source_of(ahead)
            first, count = (0, 1) if ahead == far else (1, 1) if ahead == -far else (0, TIMES)
            at = max(0, (ahead + far) * TIMES - 1)
            copies.append(
                pltpu.make_async_remote_copy(
                    src_ref=encoded.at[y, pl.ds(at, count)],
                    dst_ref=place_of(source, y, first, count),
                    send_sem=out_sent.at[y, slot], recv_sem=out_got.at[y, slot],
                    device_id={"tm": lax.rem(source + ahead + ring, ring)}, device_id_type=MESH,
                )
            )
        return copies

    reach = [way * ahead for ahead in range(far, 0, -1) for way in (1, -1)]

    def own_copy(y):
        return pltpu.make_async_copy(
            encoded.at[y, pl.ds(far * TIMES - 1, TIMES)], place_of(me, y, 0, TIMES), own_done.at[y]
        )

    def one_row(y, _):
        for stage in range(len(stages)):
            pl.when(y == stage)(functools.partial(take, stage))

        for m in range(2):
            at = m * half
            around = [patches[y, at + dt * SPAN : at + dt * SPAN + half, :] for dt in range(3)]
            total = 0.5 * dot(jnp.concatenate(around, axis=1), taps[...])
            active = (total + total * jnp.tanh(total)).astype(BF16)
            value = dot(active, merge[...]).astype(BF16)
            latent[at : at + half, :] = value
            wide = value.astype(jnp.float32)
            meansq = jnp.mean(wide * wide, axis=-1, keepdims=True)
            normed[at : at + half, :] = (wide * lax.rsqrt(meansq + 1e-06)).astype(BF16)

        tokens = dot(turn[...], normed[...]).astype(BF16)
        queries[...] = dot(tokens[plan.tokens :], w_qkv[:, :WIDTH]).astype(BF16)
        tokens = tokens[: plan.tokens]
        keys[...] = dot(tokens, w_qkv[:, WIDTH : 2 * WIDTH]).astype(BF16)
        values[...] = dot_t(values_weight[...], tokens).astype(BF16)

        def attended(part, pair):
            columns = slice(pair * 128, (pair + 1) * 128)
            rows = slice(part * group, (part + 1) * group)
            query = queries[part * some : (part + 1) * some, columns]
            both = jnp.concatenate([query * head_scale[0], query * head_scale[1]], axis=0)
            scores = jnp.where(allowed, dot_t(keys[rows, columns], both), -1e30)
            expon = jnp.exp(scores - jnp.max(scores, axis=0, keepdims=True))
            share = 1.0 / jnp.sum(expon, axis=0, keepdims=True)
            return dot(values[columns, rows], expon.astype(BF16)) * share

        for part in range(0, SPAN // 4, 2):
            for pair in range(HEADS // 2):
                left, right = attended(part, pair), attended(part + 1, pair)
                upper = jnp.where(lane < 64, left[:64], pltpu.roll(right[:64], 64, axis=1))
                lower = jnp.where(lane < 64, pltpu.roll(left[64:], 64, axis=1), right[64:])
                mixed[pair * 128 : (pair + 1) * 128, part * some : (part + 2) * some] = (
                    jnp.concatenate([upper, lower], axis=0).astype(BF16)
                )

        straight = dot_t(back[...], mixed[...]).astype(BF16)
        total = dot(straight, w_out[...]) + dot(window, latent[...])
        encoded[y] = total.astype(BF16).reshape(plan.frames, SPAN, WIDTH)

        for copy in out_copies(y, lambda ahead: me):
            copy.start()
        own_copy(y).start()
        return 0

    lax.fori_loop(0, plan.tall, one_row, 0)

    def parts_left(k, _):
        for stage in range(len(stages)):
            part_copy(stage, me, lax.rem(me + ahead_by(k), ring)).wait_send()
        return 0

    lax.fori_loop(1, ring, parts_left, 0)

    def all_done(y, _):
        for copy in out_copies(y, lambda ahead: me):
            copy.wait_send()
        for copy in out_copies(y, lambda ahead: lax.rem(me - ahead + ring, ring)):
            copy.wait_recv()
        own_copy(y).wait()
        return 0

    lax.fori_loop(0, plan.tall, all_done, 0)


def copied(value):
    def body(source, target, done):
        rows = value.shape[1]
        copies = []
        for n in range(COPIES):
            at = (n // (COPIES // 2), pl.ds(n % (COPIES // 2) * (rows // (COPIES // 2)), rows // (COPIES // 2)))
            copies.append(pltpu.make_async_copy(source.at[at], target.at[at], done.at[n]))
        for copy in copies:
            copy.start()
        for copy in copies:
            copy.wait()

    return pl.pallas_call(
        body,
        out_shape=jax.ShapeDtypeStruct(value.shape, value.dtype),
        in_specs=[pl.BlockSpec(memory_space=pltpu.VMEM)],
        out_specs=pl.BlockSpec(memory_space=pl.ANY),
        scratch_shapes=[pltpu.SemaphoreType.DMA((COPIES,))],
        compiler_params=pltpu.CompilerParams(vmem_limit_bytes=2**20),
    )(value)


def solution(mesh):
    plan = Plan(mesh.shape["tm"])
    counts = (mesh.shape["height"], mesh.shape["width"])

    def shards(video, w_conv, w_merge, w_qkv, w_out):
        operands = (video, w_conv.reshape(3, 216, 128), w_merge, w_qkv, w_out)
        dma = pltpu.SemaphoreType.DMA
        held = [pltpu.VMEM(one.shape, BF16) for one in operands]
        buffers = [
            (2, 32, COLS), (2, 32, COLS),
            (2, 16, CHANS * FRAMES * ROWS), (2, 16, CHANS * FRAMES * ROWS),
            (2, 16, 128), (4, 16, 128),
            (PARTS, plan.blocks, LINES, 128), (PARTS, plan.ring, LINES, 128),
            (plan.tall, plan.tokens + 2 * SPAN, WIDTH),
            (3 * WIDTH, WIDTH), (WIDTH, WIDTH),
            (plan.tokens, WIDTH), (plan.tokens, WIDTH),
            (plan.frames * SPAN, WIDTH), (plan.tokens, WIDTH), (WIDTH, plan.tokens),
            (WIDTH, plan.frames * SPAN),
            (plan.tall, plan.frames, SPAN, WIDTH),
            (plan.tokens + plan.frames * SPAN, plan.tokens), (plan.frames * SPAN, plan.frames * SPAN),
            (WIDTH, WIDTH),
        ]
        semaphores = [
            (len(operands),), (2,), (2,), (2,), (2,), (4,), (4,),
            (PARTS + 1, plan.ring), (PARTS + 1, plan.ring),
            (plan.tall, plan.ring // 2), (plan.tall, plan.ring // 2), (plan.tall,),
        ]
        return copied(pl.pallas_call(
            functools.partial(kernel, plan, counts),
            out_shape=pltpu.VMEM((TIMES, TALL, WIDE, WIDTH), BF16),
            in_specs=[pl.BlockSpec(memory_space=pltpu.HBM)] * len(operands),
            out_specs=pl.BlockSpec(memory_space=pl.ANY),
            scratch_shapes=held
            + [pltpu.VMEM(shape, BF16) for shape in buffers]
            + [dma(shape) for shape in semaphores],
            compiler_params=pltpu.CompilerParams(
                collective_id=0, has_side_effects=True, vmem_limit_bytes=56 * 2**20
            ),
            cost_estimate=pl.CostEstimate(
                flops=8 * 10**9, bytes_accessed=6 * 10**6, transcendentals=2 * 10**6
            ),
        )(*operands))

    return jax.shard_map(
        shards,
        mesh=mesh,
        in_specs=(P(None, "tm", "height", "width"), P(), P(), P(), P()),
        out_specs=P("tm", "height", "width", None),
        check_vma=False,
    )
```
